32 devices in a mesh: fsdp: 8 (over z, core), rep: 2 (over y), cp: 2 (over x).
Axes of the slice: x: 2, y: 2, z: 4, core: 2. Of those that a mesh axis runs over, the one named last changes fastest.
Arguments:
- block_input: bfloat16 [16, 768, 576], P(('fsdp', 'rep'), 'cp'), may hold values from -6 to 6
- segment_ids: int32 [16, 768], P(('fsdp', 'rep'), 'cp'), may hold values from 0 to 3, as said below
- attn_gain: bfloat16 [576], P('fsdp'), may hold values from 0.5 to 1.5
- w_qkv: bfloat16 [576, 960], P('fsdp'), as said below
- w_out: bfloat16 [576, 576], P('fsdp'), may hold values from -0.75 to 0.75
- mlp_gain: bfloat16 [576], P('fsdp'), may hold values from 0.5 to 1.5
- w_gate: bfloat16 [576, 1536], P('fsdp'), may hold values from -0.25 to 0.25
- w_up: bfloat16 [576, 1536], P('fsdp'), may hold values from -0.25 to 0.25
- w_down: bfloat16 [1536, 576], P('fsdp'), may hold values from -0.15625 to 0.15625
- out_cotangent: bfloat16 [16, 768, 576], P(('fsdp', 'rep'), 'cp'), may hold values from -6 to 6
Outputs:
- block_output: bfloat16 [16, 768, 576], P(('fsdp', 'rep'), 'cp')
- input_grad: float32 [16, 768, 576], P(('fsdp', 'rep'), 'cp')
- attn_gain_grad: float32 [576], P('fsdp')
- qkv_grad: float32 [576, 960], P('fsdp')
- out_grad: float32 [576, 576], P('fsdp')
- mlp_gain_grad: float32 [576], P('fsdp')
- gate_grad: float32 [576, 1536], P('fsdp')
- up_grad: float32 [576, 1536], P('fsdp')
- down_grad: float32 [1536, 576], P('fsdp')
The draws below stay inside these ranges and needn't reach their ends.
Inputs may be any that keep to these rules, and one draw needn't show every extreme that they name: `segment_ids`: along each sequence the numbers start at 0 and rise by one at each document boundary; every sequence holds 4 documents, each of 48 to 384 tokens, and exactly one of them has 384 tokens. `w_qkv`: independent entries.
All inputs are finite; a program needn't handle non-finite values.
Results may differ from the reference program's by a relative error of at most 0.011.
Values may be sent and summed in bfloat16 or wider, within the bound.
A program may use at most 128 MiB of HBM per device.

```python
import jax
import jax.numpy as jnp
from jax import lax

D = 576
QUERY_HEADS = 9
KEY_VALUE_HEADS = 3
HEAD_SIZE = 64
FF = 1536
LENGTH = 768
DOCS = 4
DOC_MOST = 384
DOC_LEAST = 48
SEQS = 16


def draw_w_qkv(key, part):
    column_span = (QUERY_HEADS + 2 * KEY_VALUE_HEADS) * HEAD_SIZE
    base = jax.random.truncated_normal(key, -6.0, 6.0, (D, column_span), jnp.float32)
    return (base * D ** (-0.5)).astype(jnp.bfloat16)


def one_packing(seq_key):
    cut_key, big_key = jax.random.split(seq_key)
    spare = LENGTH - DOC_MOST - (DOCS - 1) * DOC_LEAST
    cuts = jnp.sort(jax.random.randint(cut_key, (DOCS - 2,), 0, spare + 1))
    edges = jnp.concatenate([jnp.zeros((1,), jnp.int32), cuts.astype(jnp.int32), jnp.full((1,), spare, jnp.int32)])
    others = DOC_LEAST + (edges[1:] - edges[:-1])
    big_slot = jax.random.randint(big_key, (), 0, DOCS)
    slots = jnp.arange(DOCS, dtype=jnp.int32)
    source = jnp.clip(slots - (slots > big_slot).astype(jnp.int32), 0, DOCS - 2)
    lengths_row = jnp.where(slots == big_slot, DOC_MOST, others[source]).astype(jnp.int32)
    ends = jnp.cumsum(lengths_row)
    index_row = jnp.arange(LENGTH, dtype=jnp.int32)
    return jnp.sum((index_row[:, None] >= ends[None, :DOCS - 1]).astype(jnp.int32), axis=1)


def draw_segment_ids(key, part):
    seq_keys = jax.random.split(jax.random.fold_in(key, 11), SEQS)
    return jax.vmap(one_packing)(seq_keys).astype(jnp.int32)


def block_scale(own_key, extent, shards, least, largest):
    def one(dim, blocks):
        steps = jax.random.uniform(jax.random.fold_in(jax.random.fold_in(own_key, 6), dim), (blocks,), jnp.float32, least / len(shards), largest / len(shards))
        return jnp.repeat(jnp.exp(steps), extent[dim] // blocks).reshape((-1,) + (1,) * (len(extent) - dim - 1))

    loudness = one(*shards[0])
    for cut in shards[1:]:
        loudness = loudness * one(*cut)
    return loudness


def bell_draw(key, dims, width, most, shards=(), kind=jnp.bfloat16):
    array = jax.random.normal(key, dims, jnp.float32) * width
    if len(shards) > 0:
        array = block_scale(key, dims, shards, -0.22, 0.18) * array
    return jnp.clip(array, min=-most, max=most).astype(kind)


def setup_inputs(seed: int = 0) -> dict:
    arg_keys = jax.random.split(jax.random.key(seed), 11)
    return {
        "block_input": bell_draw(arg_keys[0], (SEQS, LENGTH, D), 1.0, 6.0, ((0, 16), (1, 2))),
        "segment_ids": draw_segment_ids(jax.random.fold_in(arg_keys[10], 71), 0),
        "attn_gain": jnp.clip(1.0 + 0.1 * jax.random.normal(arg_keys[2], (D,), jnp.float32), 0.5, 1.5).astype(jnp.bfloat16),
        "w_qkv": draw_w_qkv(jax.random.fold_in(arg_keys[10], 71), 0),
        "w_out": bell_draw(arg_keys[4], (QUERY_HEADS * HEAD_SIZE, D), (QUERY_HEADS * HEAD_SIZE // 8) ** -0.5, 0.75, ((0, 8),)),
        "mlp_gain": jnp.clip(1.0 + 0.1 * jax.random.normal(arg_keys[5], (D,), jnp.float32), 0.5, 1.5).astype(jnp.bfloat16),
        "w_gate": bell_draw(arg_keys[6], (D, FF), D ** -0.5, 0.25, ((0, 8),)),
        "w_up": bell_draw(arg_keys[7], (D, FF), D ** -0.5, 0.25, ((0, 8),)),
        "w_down": bell_draw(arg_keys[8], (FF, D), FF ** -0.5, 0.15625, ((0, 8),)),
        "out_cotangent": bell_draw(arg_keys[9], (SEQS, LENGTH, D), 1.0, 6.0, ((0, 16), (1, 2))),
    }


EPS = 1e-05
THETA = 100000.0
MASKED = -1e+30

def rope_tables(positions):
    half = HEAD_SIZE // 2
    freq = THETA ** (-2.0 * jnp.arange(half, dtype=jnp.float32) / HEAD_SIZE)
    angle = positions.astype(jnp.float32)[:, None] * freq[None, :]
    return (jnp.cos(angle), jnp.sin(angle))

def apply_rotation(tensor, cosine_table, sine_table, direction):
    half = HEAD_SIZE // 2
    first = tensor[..., :half]
    second = tensor[..., half:]
    cos_b = cosine_table[:, None, :]
    sin_b = sine_table[:, None, :] * direction
    return jnp.concatenate([first * cos_b - second * sin_b, first * sin_b + second * cos_b], axis=-1)

def doc_positions(seg_row):
    index_row = jnp.arange(seg_row.shape[0], dtype=jnp.int32)
    starts = lax.optimization_barrier(jnp.sum((seg_row[None, :] < seg_row[:, None]).astype(jnp.int32), axis=1))
    return index_row - starts

def norm_forward(values, gain):
    inv_rms = lax.rsqrt(lax.optimization_barrier(jnp.mean(values * values, axis=-1, keepdims=True)) + EPS)
    normed = values * inv_rms
    return (normed, inv_rms, (normed * gain.astype(jnp.float32)).astype(jnp.bfloat16))

def norm_backward(d_normed, normed, inv_rms, gain):
    gain_grad = lax.optimization_barrier(jnp.sum(d_normed * normed, axis=0))
    scaled = d_normed * gain.astype(jnp.float32)
    return (gain_grad, inv_rms * (scaled - normed * lax.optimization_barrier(jnp.mean(scaled * normed, axis=-1, keepdims=True))))

def score_block(query_rows, keys_three_axis, visible):
    row_span = query_rows.shape[0]
    grouped_heads = query_rows.reshape(row_span, KEY_VALUE_HEADS, QUERY_HEADS // KEY_VALUE_HEADS, HEAD_SIZE).astype(jnp.float32)
    scores = jnp.einsum('nkgd,mkd->kgnm', grouped_heads, keys_three_axis.astype(jnp.float32)) * HEAD_SIZE ** (-0.5)
    return jnp.where(visible[None, None], scores, MASKED)

def attend(query_rows, keys_three_axis, values_three_axis, visible):
    row_span = query_rows.shape[0]
    scores = score_block(query_rows, keys_three_axis, visible)
    top = lax.optimization_barrier(jnp.max(scores, axis=-1, keepdims=True))
    expo = jnp.exp(scores - top)
    total = lax.optimization_barrier(jnp.sum(expo, axis=-1, keepdims=True))
    probs = (expo / total).astype(jnp.bfloat16)
    log_total = top + jnp.log(total)
    mixed_heads = jnp.einsum('kgnm,mkd->nkgd', probs.astype(jnp.float32), values_three_axis.astype(jnp.float32))
    return (mixed_heads.reshape(row_span, QUERY_HEADS * HEAD_SIZE).astype(jnp.bfloat16), log_total)

def attend_back(mixed_gradient, mixed_heads, query_rows, keys_three_axis, values_three_axis, visible, log_total):
    row_span = query_rows.shape[0]
    query_group = QUERY_HEADS // KEY_VALUE_HEADS
    scores = score_block(query_rows, keys_three_axis, visible)
    probs = jnp.exp(scores - log_total)
    probs_b = probs.astype(jnp.bfloat16).astype(jnp.float32)
    grouped_gradient = mixed_gradient.reshape(row_span, KEY_VALUE_HEADS, query_group, HEAD_SIZE).astype(jnp.float32)
    d_values = jnp.einsum('kgnm,nkgd->mkd', probs_b, grouped_gradient)
    d_probs = jnp.einsum('nkgd,mkd->kgnm', grouped_gradient, values_three_axis.astype(jnp.float32))
    change_amount = lax.optimization_barrier(jnp.sum(grouped_gradient * mixed_heads.reshape(row_span, KEY_VALUE_HEADS, query_group, HEAD_SIZE).astype(jnp.float32), axis=-1))
    change_amount = jnp.transpose(change_amount, (1, 2, 0))[..., None]
    d_scores = (probs * (d_probs - change_amount)).astype(jnp.bfloat16).astype(jnp.float32)
    grouped_heads = query_rows.reshape(row_span, KEY_VALUE_HEADS, query_group, HEAD_SIZE).astype(jnp.float32)
    d_queries = jnp.einsum('kgnm,mkd->nkgd', d_scores, keys_three_axis.astype(jnp.float32)) * HEAD_SIZE ** (-0.5)
    d_keys = jnp.einsum('kgnm,nkgd->mkd', d_scores, grouped_heads) * HEAD_SIZE ** (-0.5)
    return (d_queries.reshape(row_span, QUERY_HEADS, HEAD_SIZE), d_keys, d_values)

def one_sequence(seq_input, seq_ids, seq_cot, weights):
    attn_gain, w_qkv, w_out, mlp_gain, w_gate, w_up, w_down = weights
    every_length = seq_input.shape[0]
    query_columns = QUERY_HEADS * HEAD_SIZE
    key_columns = KEY_VALUE_HEADS * HEAD_SIZE
    residual = seq_input.astype(jnp.float32)
    positions = doc_positions(seq_ids)
    index_row = jnp.arange(every_length, dtype=jnp.int32)
    visible = (seq_ids[None, :] == seq_ids[:, None]) & (index_row[None, :] <= index_row[:, None])
    cosine_table, sine_table = rope_tables(positions)
    normed1, inv_rms1, xn = norm_forward(residual, attn_gain)
    output_projection = jnp.dot(xn, w_qkv, preferred_element_type=jnp.float32)
    query_rows = apply_rotation(output_projection[:, :query_columns].reshape(every_length, QUERY_HEADS, HEAD_SIZE), cosine_table, sine_table, 1.0).astype(jnp.bfloat16)
    keys_three_axis = apply_rotation(output_projection[:, query_columns:query_columns + key_columns].reshape(every_length, KEY_VALUE_HEADS, HEAD_SIZE), cosine_table, sine_table, 1.0).astype(jnp.bfloat16)
    values_three_axis = output_projection[:, query_columns + key_columns:].astype(jnp.bfloat16).reshape(every_length, KEY_VALUE_HEADS, HEAD_SIZE)
    attn_mix, log_total = attend(query_rows, keys_three_axis, values_three_axis, visible)
    mid = residual + jnp.dot(attn_mix, w_out, preferred_element_type=jnp.float32)
    normed2, inv_rms2, hidden_n = norm_forward(mid, mlp_gain)
    gate = jnp.dot(hidden_n, w_gate, preferred_element_type=jnp.float32)
    up_val = jnp.dot(hidden_n, w_up, preferred_element_type=jnp.float32)
    sigma = jax.nn.sigmoid(gate)
    silu_gate = gate * sigma
    act = (silu_gate * up_val).astype(jnp.bfloat16)
    block_output = (mid + jnp.dot(act, w_down, preferred_element_type=jnp.float32)).astype(jnp.bfloat16)
    cot_f = seq_cot.astype(jnp.float32)
    d_act = jnp.dot(seq_cot, w_down.T, preferred_element_type=jnp.float32)
    down_grad = jnp.dot(act.T, seq_cot, preferred_element_type=jnp.float32)
    d_gate = (d_act * up_val * sigma * (1.0 + gate * (1.0 - sigma))).astype(jnp.bfloat16)
    d_up = (d_act * silu_gate).astype(jnp.bfloat16)
    gate_grad = jnp.dot(hidden_n.T, d_gate, preferred_element_type=jnp.float32)
    up_grad = jnp.dot(hidden_n.T, d_up, preferred_element_type=jnp.float32)
    d_hn = jnp.dot(d_gate, w_gate.T, preferred_element_type=jnp.float32) + jnp.dot(d_up, w_up.T, preferred_element_type=jnp.float32)
    mlp_gain_grad, d_norm2 = norm_backward(d_hn, normed2, inv_rms2, mlp_gain)
    d_mid = cot_f + d_norm2
    d_mid_b = d_mid.astype(jnp.bfloat16)
    out_grad = jnp.dot(attn_mix.T, d_mid_b, preferred_element_type=jnp.float32)
    d_attn = jnp.dot(d_mid_b, w_out.T, preferred_element_type=jnp.float32).astype(jnp.bfloat16)
    d_queries, d_keys, d_values = attend_back(d_attn, attn_mix, query_rows, keys_three_axis, values_three_axis, visible, log_total)
    d_proj = jnp.concatenate([apply_rotation(d_queries, cosine_table, sine_table, -1.0).reshape(every_length, query_columns), apply_rotation(d_keys, cosine_table, sine_table, -1.0).reshape(every_length, key_columns), d_values.reshape(every_length, key_columns)], axis=1).astype(jnp.bfloat16)
    qkv_grad = jnp.dot(xn.T, d_proj, preferred_element_type=jnp.float32)
    d_xn = jnp.dot(d_proj, w_qkv.T, preferred_element_type=jnp.float32)
    attn_gain_grad, d_norm1 = norm_backward(d_xn, normed1, inv_rms1, attn_gain)
    input_grad = d_mid + d_norm1
    grads = (attn_gain_grad, qkv_grad, out_grad, mlp_gain_grad, gate_grad, up_grad, down_grad)
    return (block_output, input_grad, grads)

def reference(block_input, segment_ids, attn_gain, w_qkv, w_out, mlp_gain, w_gate, w_up, w_down, out_cotangent):
    weights = (attn_gain, w_qkv, w_out, mlp_gain, w_gate, w_up, w_down)
    zero_grads = tuple((jnp.zeros(weight.shape, jnp.float32) for weight in weights))

    def step(carry, item):
        seq_input, seq_ids, seq_cot = item
        block_output, input_grad, grads = one_sequence(seq_input, seq_ids, seq_cot, weights)
        return (tuple((total + grad for total, grad in zip(carry, grads))), (block_output, input_grad))
    grads, (outputs, input_grads) = lax.scan(step, zero_grads, (block_input, segment_ids, out_cotangent))
    return (outputs, input_grads, grads[0], grads[1], grads[2], grads[3], grads[4], grads[5], grads[6])
```

```python
import functools

import jax
import jax.numpy as jnp
from jax import lax
from jax.experimental import pallas as pl
from jax.experimental.pallas import tpu as pltpu
from jax.sharding import PartitionSpec as P

QUERY_HEADS = 9
KEY_VALUE_HEADS = 3
HEAD_SIZE = 64


EPS = 1e-05
THETA = 100000.0
MASKED = -1e30

VMEM_BYTES = 50 * 1024 * 1024
MESH_ID = pl.DeviceIdType.MESH


def gather_kernel(depth, count, *refs):
    ins, outs = refs[:count], refs[count : 2 * count]
    own_sem, up_sem, down_sem, arrive_sem, core_sem, core_arrive = refs[2 * count :]
    me = lax.axis_index("fsdp")
    z, core = me // 2, me % 2
    partner = 2 * z + 1 - core
    barrier = pltpu.get_barrier_semaphore()
    pl.semaphore_signal(barrier, inc=1, device_id={"fsdp": partner}, device_id_type=MESH_ID)

    @pl.when(z > 0)
    def _():
        pl.semaphore_signal(barrier, inc=1, device_id={"fsdp": me - 2}, device_id_type=MESH_ID)

    @pl.when(z < depth - 1)
    def _():
        pl.semaphore_signal(barrier, inc=1, device_id={"fsdp": me + 2}, device_id_type=MESH_ID)

    has_down, has_up = jnp.where(z > 0, 1, 0), jnp.where(z < depth - 1, 1, 0)
    pl.semaphore_wait(barrier, 1 + has_down + has_up)

    def own(k):
        return pltpu.make_async_copy(ins[k], outs[k].at[me], own_sem.at[k])

    def along(k, shard, step, sems, source=None):
        place = outs[k].at[2 * shard + core]
        return pltpu.make_async_remote_copy(
            src_ref=place if source is None else source,
            dst_ref=place,
            send_sem=sems.at[k, shard],
            recv_sem=arrive_sem.at[k, shard],
            device_id={"fsdp": me + 2 * step},
            device_id_type=MESH_ID,
        )

    def across(k, shard, parity, source=None):
        place = outs[k].at[2 * shard + parity]
        return pltpu.make_async_remote_copy(
            src_ref=place if source is None else source,
            dst_ref=place,
            send_sem=core_sem.at[k, shard],
            recv_sem=core_arrive.at[k, shard],
            device_id={"fsdp": partner},
            device_id_type=MESH_ID,
        )

    for k in range(count):
        own(k).start()

        @pl.when(z < depth - 1)
        def _():
            along(k, z, 1, up_sem, ins[k]).start()

        @pl.when(z > 0)
        def _():
            along(k, z, -1, down_sem, ins[k]).start()

        across(k, z, core, ins[k]).start()
    for k in range(count):
        for step in range(1, depth):
            below, above = z - step, z + step

            @pl.when(below >= 0)
            def _():
                along(k, below, 1, up_sem).wait_recv()

                @pl.when(z < depth - 1)
                def _():
                    along(k, below, 1, up_sem).start()

                across(k, below, core).start()

            @pl.when(above < depth)
            def _():
                along(k, above, -1, down_sem).wait_recv()

                @pl.when(z > 0)
                def _():
                    along(k, above, -1, down_sem).start()

                across(k, above, core).start()

    for k in range(count):
        own(k).wait()
        for shard in range(depth):
            across(k, shard, 1 - core).wait_recv()
            across(k, shard, core).wait_send()

            @pl.when((shard <= z) & (z < depth - 1))
            def _():
                along(k, shard, 1, up_sem).wait_send()

            @pl.when((shard >= z) & (z > 0))
            def _():
                along(k, shard, -1, down_sem).wait_send()


def gather_shards(arrays, ways):
    count, depth = len(arrays), ways // 2
    return pl.pallas_call(
        functools.partial(gather_kernel, depth, count),
        out_shape=[jax.ShapeDtypeStruct((ways,) + a.shape, a.dtype) for a in arrays],
        in_specs=[pl.BlockSpec(memory_space=pltpu.VMEM)] * count,
        out_specs=[pl.BlockSpec(memory_space=pltpu.VMEM)] * count,
        scratch_shapes=[pltpu.SemaphoreType.DMA((count,))]
        + [pltpu.SemaphoreType.DMA((count, depth))] * 5,
        compiler_params=pltpu.CompilerParams(
            collective_id=1, has_side_effects=True, vmem_limit_bytes=VMEM_BYTES
        ),
    )(*arrays)


def part_of(ref, lead, index, parts):
    rows, columns = ref.shape[-2:]
    if columns % (4 * 128) == 0:
        size = columns // parts
        return ref.at[lead, :, pl.ds(pl.multiple_of(index * size, size), size)]
    size = rows // parts
    return ref.at[lead, pl.ds(pl.multiple_of(index * size, size), size), :]


def reduce_kernel(depth, count, *refs):
    parts, outs = refs[:count], refs[count : 2 * count]
    rest = refs[2 * count :]
    first, second, third, fourth, held, quarter, joined = [
        rest[i * count : (i + 1) * count] for i in range(7)
    ]
    send0, recv0, send1, recv1, send2, recv2, send3, recv3, send4, recv4 = rest[7 * count :]
    me, x, y = lax.axis_index("fsdp"), lax.axis_index("cp"), lax.axis_index("rep")
    z, core = me // 2, me % 2
    partner = 2 * z + 1 - core
    f32 = jnp.float32

    barrier = pltpu.get_barrier_semaphore()
    others = [{"fsdp": partner}, {"cp": 1 - x}, {"rep": 1 - y}, {"cp": 1 - x, "rep": 1 - y}]
    others += [{"fsdp": 2 * ((z + s) % depth) + core} for s in range(1, depth)]
    for other in others:
        pl.semaphore_signal(barrier, inc=1, device_id=other, device_id_type=MESH_ID)
    pl.semaphore_wait(barrier, len(others))

    def remote(source, place, send, recv, device):
        return pltpu.make_async_remote_copy(
            src_ref=source,
            dst_ref=place,
            send_sem=send,
            recv_sem=recv,
            device_id=device,
            device_id_type=MESH_ID,
        )

    def copy0(k, j):
        return remote(
            parts[k].at[2 * j + 1 - core],
            first[k].at[j],
            send0.at[k, j],
            recv0.at[k, j],
            {"fsdp": partner},
        )

    def axes(j):
        return (x, y, "cp", "rep") if j % 2 == 0 else (y, x, "rep", "cp")

    def copy1(k, j):
        own1, _, name1, _ = axes(j)
        return remote(
            part_of(held[k], j, 1 - own1, 2),
            second[k].at[j],
            send1.at[k, j],
            recv1.at[k, j],
            {name1: 1 - own1},
        )

    def copy2(k, j):
        own1, own2, _, name2 = axes(j)
        return remote(
            part_of(held[k], j, own1 * 2 + 1 - own2, 4),
            third[k].at[j],
            send2.at[k, j],
            recv2.at[k, j],
            {name2: 1 - own2},
        )

    def copy3(k, step):
        to = (z + step) % depth
        return remote(
            quarter[k].at[to],
            fourth[k].at[step],
            send3.at[k, step],
            recv3.at[k, step],
            {"fsdp": 2 * to + core},
        )

    mine = jnp.where(z % 2 == 0, x * 2 + y, y * 2 + x)

    def copy4(k, which):
        place = part_of(joined[k], 0, mine, 4)
        device = [{"cp": 1 - x}, {"rep": 1 - y}, {"cp": 1 - x, "rep": 1 - y}][which]
        return remote(place, place, send4.at[k, which], recv4.at[k, which], device)

    for k in range(count):
        for j in range(depth):
            copy0(k, j).start()
    for k in range(count):
        for j in range(depth):
            copy0(k, j).wait_recv()
            total = parts[k][2 * j + core].astype(f32) + first[k][j].astype(f32)
            held[k][j] = total.astype(held[k].dtype)
            copy1(k, j).start()
    for k in range(count):
        for j in range(depth):
            own1, own2, _, _ = axes(j)
            copy1(k, j).wait_recv()
            half = part_of(held[k], j, own1, 2)
            half[...] = (half[...].astype(f32) + second[k][j].astype(f32)).astype(half.dtype)
            copy2(k, j).start()
    for k in range(count):
        for j in range(depth):
            own1, own2, _, _ = axes(j)
            copy2(k, j).wait_recv()
            piece = part_of(held[k], j, own1 * 2 + own2, 4)
            total = piece[...].astype(f32) + third[k][j].astype(f32)
            quarter[k][j] = total.astype(quarter[k].dtype)
        for step in range(1, depth):
            copy3(k, step).start()
    for k in range(count):
        total = quarter[k][z].astype(f32)
        for step in range(1, depth):
            copy3(k, step).wait_recv()
            total = total + fourth[k][step].astype(f32)
        place = part_of(joined[k], 0, mine, 4)
        place[...] = total.astype(place.dtype)
        for which in range(3):
            copy4(k, which).start()
    for k in range(count):
        for which in range(3):
            copy4(k, which).wait_recv()
        outs[k][...] = joined[k][0].astype(f32)
    for k in range(count):
        for j in range(depth):
            copy0(k, j).wait_send()
            copy1(k, j).wait_send()
            copy2(k, j).wait_send()
        for step in range(1, depth):
            copy3(k, step).wait_send()
        for which in range(3):
            copy4(k, which).wait_send()


def reduce_shards(arrays):
    count, ways = len(arrays), arrays[0].shape[0]
    depth = ways // 2
    kind = arrays[0].dtype
    wholes = [(depth,) + a.shape[1:] for a in arrays]
    halves, quarters = [], []
    for a in arrays:
        rows, columns = a.shape[1:]
        by_columns = columns % (4 * 128) == 0
        halves.append((depth, rows, columns // 2) if by_columns else (depth, rows // 2, columns))
        quarters.append((depth, rows, columns // 4) if by_columns else (depth, rows // 4, columns))
    buffers = []
    for shapes in (wholes, halves, quarters, quarters, wholes, quarters):
        buffers += [pltpu.VMEM(s, kind) for s in shapes]
    buffers += [pltpu.VMEM((1,) + a.shape[1:], kind) for a in arrays]
    sems = [pltpu.SemaphoreType.DMA((count, depth))] * 8 + [pltpu.SemaphoreType.DMA((count, 3))] * 2
    return pl.pallas_call(
        functools.partial(reduce_kernel, depth, count),
        out_shape=[jax.ShapeDtypeStruct(a.shape[1:], jnp.float32) for a in arrays],
        in_specs=[pl.BlockSpec(memory_space=pltpu.VMEM)] * count,
        out_specs=[pl.BlockSpec(memory_space=pltpu.VMEM)] * count,
        scratch_shapes=buffers + sems,
        compiler_params=pltpu.CompilerParams(
            collective_id=2, has_side_effects=True, vmem_limit_bytes=VMEM_BYTES
        ),
    )(*arrays)


def rope_tables(positions):
    half = HEAD_SIZE // 2
    freq = THETA ** (-2.0 * jnp.arange(half, dtype=jnp.float32) / HEAD_SIZE)
    angle = positions.astype(jnp.float32)[:, None] * freq[None, :]
    return (jnp.cos(angle), jnp.sin(angle))


def apply_rotation(tensor, cosine_table, sine_table, direction):
    half = HEAD_SIZE // 2
    first = tensor[..., :half]
    second = tensor[..., half:]
    cos_b = cosine_table[:, None, :]
    sin_b = sine_table[:, None, :] * direction
    return jnp.concatenate(
        [first * cos_b - second * sin_b, first * sin_b + second * cos_b], axis=-1
    )


def doc_positions(seg_row):
    index_row = jnp.arange(seg_row.shape[0], dtype=jnp.int32)
    starts = jnp.sum((seg_row[None, :] < seg_row[:, None]).astype(jnp.int32), axis=1)
    return index_row - starts


def times_transposed(left, right):
    return lax.dot_general(
        left, right, (((1,), (1,)), ((), ())), preferred_element_type=jnp.float32
    )


def transposed_times(left, right):
    return lax.dot_general(
        left, right, (((0,), (0,)), ((), ())), preferred_element_type=jnp.float32
    )


def norm_forward(values, gain):
    inv_rms = lax.rsqrt(jnp.mean(values * values, axis=-1, keepdims=True) + EPS)
    normed = values * inv_rms
    return (normed, inv_rms, (normed * gain.astype(jnp.float32)).astype(jnp.bfloat16))


def norm_backward(d_normed, normed, inv_rms, gain):
    gain_grad = jnp.sum(d_normed * normed, axis=0)
    scaled = d_normed * gain.astype(jnp.float32)
    return (
        gain_grad,
        inv_rms * (scaled - normed * jnp.mean(scaled * normed, axis=-1, keepdims=True)),
    )


def score_block(query_rows, keys_three_axis, visible):
    row_span = query_rows.shape[0]
    grouped_heads = query_rows.reshape(
        row_span, KEY_VALUE_HEADS, QUERY_HEADS // KEY_VALUE_HEADS, HEAD_SIZE
    )
    scores = jnp.einsum(
        "nkgd,mkd->kgnm", grouped_heads, keys_three_axis, preferred_element_type=jnp.float32
    ) * HEAD_SIZE ** (-0.5)
    return jnp.where(visible[None, None], scores, MASKED)


def attend(query_rows, keys_three_axis, values_three_axis, visible):
    row_span = query_rows.shape[0]
    scores = score_block(query_rows, keys_three_axis, visible)
    top = jnp.max(scores, axis=-1, keepdims=True)
    expo = jnp.exp(scores - top)
    total = jnp.sum(expo, axis=-1, keepdims=True)
    probs = (expo / total).astype(jnp.bfloat16)
    log_total = top + jnp.log(total)
    mixed_heads = jnp.einsum(
        "kgnm,mkd->nkgd", probs, values_three_axis, preferred_element_type=jnp.float32
    )
    return (mixed_heads.reshape(row_span, QUERY_HEADS * HEAD_SIZE).astype(jnp.bfloat16), log_total)


def attend_back(
    mixed_gradient, mixed_heads, query_rows, keys_three_axis, values_three_axis, visible, log_total
):
    row_span = query_rows.shape[0]
    query_group = QUERY_HEADS // KEY_VALUE_HEADS
    scores = score_block(query_rows, keys_three_axis, visible)
    probs = jnp.exp(scores - log_total)
    probs_b = probs.astype(jnp.bfloat16)
    grouped_gradient = mixed_gradient.reshape(row_span, KEY_VALUE_HEADS, query_group, HEAD_SIZE)
    d_values = jnp.einsum(
        "kgnm,nkgd->mkd", probs_b, grouped_gradient, preferred_element_type=jnp.float32
    )
    d_probs = jnp.einsum(
        "nkgd,mkd->kgnm", grouped_gradient, values_three_axis, preferred_element_type=jnp.float32
    )
    change_amount = jnp.sum(
        grouped_gradient.astype(jnp.float32)
        * mixed_heads.reshape(row_span, KEY_VALUE_HEADS, query_group, HEAD_SIZE).astype(
            jnp.float32
        ),
        axis=-1,
    )
    change_amount = jnp.transpose(change_amount, (1, 2, 0))[..., None]
    d_scores = (probs * (d_probs - change_amount)).astype(jnp.bfloat16)
    grouped_heads = query_rows.reshape(row_span, KEY_VALUE_HEADS, query_group, HEAD_SIZE)
    d_queries = jnp.einsum(
        "kgnm,mkd->nkgd", d_scores, keys_three_axis, preferred_element_type=jnp.float32
    ) * HEAD_SIZE ** (-0.5)
    d_keys = jnp.einsum(
        "kgnm,nkgd->mkd", d_scores, grouped_heads, preferred_element_type=jnp.float32
    ) * HEAD_SIZE ** (-0.5)
    return (d_queries.reshape(row_span, QUERY_HEADS, HEAD_SIZE), d_keys, d_values)


def swap_halves(value):
    return lax.ppermute(value, "cp", [(0, 1), (1, 0)])


def both_halves(value, axis):
    other = swap_halves(value)
    first = lax.axis_index("cp") == 0
    return jnp.concatenate(
        [jnp.where(first, value, other), jnp.where(first, other, value)], axis=axis
    )


def shards(
    ways, copies, block_input, segment_ids, attn_gain, w_qkv, w_out, mlp_gain, w_gate, w_up, w_down, out_cotangent
):
    residual = block_input[0].astype(jnp.float32)
    row_span = residual.shape[0]
    query_columns = QUERY_HEADS * HEAD_SIZE
    key_columns = KEY_VALUE_HEADS * HEAD_SIZE
    gains = jnp.zeros((16, 128), jnp.bfloat16)
    gains = gains.at[0, : attn_gain.shape[0]].set(attn_gain).at[1, : mlp_gain.shape[0]].set(mlp_gain)
    gathered = gather_shards([w_qkv, w_out, gains, w_gate, w_up, w_down], ways)
    qkv_full, out_full, gate_full, up_full, down_full = [
        gathered[i].reshape(-1, gathered[i].shape[-1]) for i in (0, 1, 3, 4, 5)
    ]
    gain_a = gathered[2][:, 0, : attn_gain.shape[0]].reshape(-1)
    gain_m = gathered[2][:, 1, : mlp_gain.shape[0]].reshape(-1)
    whole_ids = both_halves(segment_ids, 1)[0]
    every_length = whole_ids.shape[0]
    offset = lax.axis_index("cp") * row_span
    key_index = jnp.arange(every_length, dtype=jnp.int32)
    key_positions = doc_positions(whole_ids)
    query_index = offset + jnp.arange(row_span, dtype=jnp.int32)
    query_positions = lax.dynamic_slice_in_dim(key_positions, offset, row_span)
    local_ids = segment_ids[0]
    visible = (whole_ids[None, :] == local_ids[:, None]) & (
        key_index[None, :] <= query_index[:, None]
    )
    query_cosine, query_sine = rope_tables(query_positions)
    k_cos, k_sin = rope_tables(key_positions)
    normed1, inv_rms1, xn = norm_forward(residual, gain_a)
    output_projection = jnp.dot(xn, qkv_full, preferred_element_type=jnp.float32)
    query_rows = apply_rotation(
        output_projection[:, :query_columns].reshape(row_span, QUERY_HEADS, HEAD_SIZE),
        query_cosine,
        query_sine,
        1.0,
    ).astype(jnp.bfloat16)
    keys_local = (
        apply_rotation(
            output_projection[:, query_columns : query_columns + key_columns].reshape(
                row_span, KEY_VALUE_HEADS, HEAD_SIZE
            ),
            query_cosine,
            query_sine,
            1.0,
        )
        .astype(jnp.bfloat16)
        .reshape(row_span, key_columns)
    )
    values_local = output_projection[:, query_columns + key_columns :].astype(jnp.bfloat16)
    every_pair = both_halves(jnp.concatenate([keys_local, values_local], axis=1), 0)
    every_key, every_value = every_pair[:, :key_columns], every_pair[:, key_columns:]
    keys_three_axis = every_key.reshape(every_length, KEY_VALUE_HEADS, HEAD_SIZE)
    values_three_axis = every_value.reshape(every_length, KEY_VALUE_HEADS, HEAD_SIZE)
    attn_mix, log_total = attend(query_rows, keys_three_axis, values_three_axis, visible)
    mid = residual + jnp.dot(attn_mix, out_full, preferred_element_type=jnp.float32)
    normed2, inv_rms2, hidden_n = norm_forward(mid, gain_m)
    gate = jnp.dot(hidden_n, gate_full, preferred_element_type=jnp.float32)
    up_val = jnp.dot(hidden_n, up_full, preferred_element_type=jnp.float32)
    sigma = jax.nn.sigmoid(gate)
    silu_gate = gate * sigma
    act = (silu_gate * up_val).astype(jnp.bfloat16)
    block_output = (mid + jnp.dot(act, down_full, preferred_element_type=jnp.float32)).astype(
        jnp.bfloat16
    )
    cotangent = out_cotangent[0]
    d_act = times_transposed(cotangent, down_full)
    down_grad = transposed_times(act, cotangent)
    d_gate = (d_act * up_val * sigma * (1.0 + gate * (1.0 - sigma))).astype(jnp.bfloat16)
    d_up = (d_act * silu_gate).astype(jnp.bfloat16)
    gate_grad = transposed_times(hidden_n, d_gate)
    up_grad = transposed_times(hidden_n, d_up)
    d_hn = times_transposed(d_gate, gate_full) + times_transposed(d_up, up_full)
    mlp_gain_grad, d_norm2 = norm_backward(d_hn, normed2, inv_rms2, gain_m)
    d_mid = cotangent.astype(jnp.float32) + d_norm2
    d_mid_b = d_mid.astype(jnp.bfloat16)
    out_grad = transposed_times(attn_mix, d_mid_b)
    d_attn = times_transposed(d_mid_b, out_full).astype(jnp.bfloat16)
    d_queries, d_keys, d_values = attend_back(
        d_attn, attn_mix, query_rows, keys_three_axis, values_three_axis, visible, log_total
    )
    d_keys_flat = apply_rotation(d_keys, k_cos, k_sin, -1.0).reshape(every_length, key_columns)
    d_values_flat = d_values.reshape(every_length, key_columns)
    pair = jnp.concatenate([d_keys_flat, d_values_flat], axis=1)
    away = lax.dynamic_slice_in_dim(pair, row_span - offset, row_span)
    pair_part = lax.dynamic_slice_in_dim(pair, offset, row_span) + swap_halves(
        away.astype(jnp.bfloat16)
    ).astype(jnp.float32)
    d_proj = jnp.concatenate(
        [
            apply_rotation(d_queries, query_cosine, query_sine, -1.0).reshape(
                row_span, query_columns
            ),
            pair_part,
        ],
        axis=1,
    ).astype(jnp.bfloat16)
    qkv_grad = transposed_times(xn, d_proj)
    d_xn = times_transposed(d_proj, qkv_full)
    attn_gain_grad, d_norm1 = norm_backward(d_xn, normed1, inv_rms1, gain_a)
    input_grad = d_mid + d_norm1
    if copies == (2, 2):
        bf16 = jnp.bfloat16
        shard = attn_gain.shape[0]
        gain_grads = jnp.stack(
            [attn_gain_grad.reshape(ways, shard), mlp_gain_grad.reshape(ways, shard)], axis=1
        )
        gain_grads = jnp.pad(gain_grads, ((0, 0), (0, 14), (0, 512 - shard))).astype(bf16)
        both = jnp.concatenate([qkv_grad.astype(bf16), out_grad.astype(bf16)], axis=1)
        stacked = [
            g.astype(bf16).reshape(ways, -1, g.shape[-1])
            for g in (gate_grad, up_grad, down_grad, both)
        ]
        gate_s, up_s, down_s, both_s, gain_s = reduce_shards(stacked + [gain_grads])
        qkv_s, out_s = both_s[:, : w_qkv.shape[1]], both_s[:, w_qkv.shape[1] :]
        gain_a_s, gain_m_s = gain_s[0, :shard], gain_s[1, :shard]
    else:
        grads = (attn_gain_grad, qkv_grad, out_grad, mlp_gain_grad, gate_grad, up_grad, down_grad)
        grads = [lax.psum_scatter(g, "fsdp", scatter_dimension=0, tiled=True) for g in grads]
        gain_a_s, qkv_s, out_s, gain_m_s, gate_s, up_s, down_s = lax.psum(grads, ("rep", "cp"))
    return (
        block_output[None],
        input_grad[None],
        gain_a_s,
        qkv_s,
        out_s,
        gain_m_s,
        gate_s,
        up_s,
        down_s,
    )


def solution(mesh):
    ways = mesh.shape["fsdp"]
    copies = (mesh.shape["rep"], mesh.shape["cp"])
    return jax.shard_map(
        functools.partial(shards, ways, copies),
        mesh=mesh,
        in_specs=(
            P(("fsdp", "rep"), "cp", None),
            P(("fsdp", "rep"), "cp"),
            P("fsdp"),
            P("fsdp", None),
            P("fsdp", None),
            P("fsdp"),
            P("fsdp", None),
            P("fsdp", None),
            P("fsdp", None),
            P(("fsdp", "rep"), "cp", None),
        ),
        out_specs=(
            P(("fsdp", "rep"), "cp", None),
            P(("fsdp", "rep"), "cp", None),
            P("fsdp"),
            P("fsdp", None),
            P("fsdp", None),
            P("fsdp"),
            P("fsdp", None),
            P("fsdp", None),
            P("fsdp", None),
        ),
        check_vma=False,
    )
```

```python
import functools

import jax
import jax.numpy as jnp
from jax import lax
from jax.experimental import pallas as pl
from jax.experimental.pallas import tpu as pltpu
from jax.sharding import PartitionSpec as P

QUERY_HEADS = 9
KEY_VALUE_HEADS = 3
HEAD_SIZE = 64


EPS = 1e-05
THETA = 100000.0
MASKED = -1e30

VMEM_BYTES = 50 * 1024 * 1024
MESH_ID = pl.DeviceIdType.MESH


def part_of(ref, lead, index, parts):
    rows, columns = ref.shape[-2:]
    if columns % (4 * 128) == 0:
        size = columns // parts
        return ref.at[lead, :, pl.ds(pl.multiple_of(index * size, size), size)]
    size = rows // parts
    return ref.at[lead, pl.ds(pl.multiple_of(index * size, size), size), :]


def gather_kernel(depth, count, *refs):
    ins, outs = refs[:count], refs[count : 2 * count]
    own_sem, z_send, z_recv, send1, recv1, send2, recv2, core_send, core_recv = refs[2 * count :]
    me, x, y = lax.axis_index("fsdp"), lax.axis_index("cp"), lax.axis_index("rep")
    z, core = me // 2, me % 2
    partner = 2 * z + 1 - core
    barrier = pltpu.get_barrier_semaphore()
    others = [{"fsdp": partner}, {"cp": 1 - x}, {"rep": 1 - y}]
    others += [{"fsdp": 2 * ((z + s) % depth) + core} for s in range(1, depth)]
    for other in others:
        pl.semaphore_signal(barrier, inc=1, device_id=other, device_id_type=MESH_ID)
    pl.semaphore_wait(barrier, len(others))

    def remote(source, place, send, recv, device):
        return pltpu.make_async_remote_copy(
            src_ref=source,
            dst_ref=place,
            send_sem=send,
            recv_sem=recv,
            device_id=device,
            device_id_type=MESH_ID,
        )

    def axes(j):
        return (x, y, "cp", "rep") if j % 2 == 0 else (y, x, "rep", "cp")

    def own(k):
        return pltpu.make_async_copy(ins[k].at[0], outs[k].at[me], own_sem.at[k])

    def outward(k, step):
        mine = jnp.where(z % 2 == 0, y * 2 + x, x * 2 + y)
        return remote(
            part_of(ins[k], 0, mine, 4),
            part_of(outs[k], me, mine, 4),
            z_send.at[k, step],
            z_recv.at[k, step],
            {"fsdp": 2 * ((z + step) % depth) + core},
        )

    def inward(k, step):
        shard = (z + depth - step) % depth
        even = shard % 2 == 0
        mine = jnp.where(even, y * 2 + x, x * 2 + y)
        place = part_of(outs[k], 2 * shard + core, mine, 4)
        return remote(place, place, z_send.at[k, step], z_recv.at[k, step], {"fsdp": partner})

    def joins(k, shard, which):
        own1, own2, name1, name2 = axes(shard)
        if which == 0:
            quarter = part_of(outs[k], 2 * shard + core, own2 * 2 + own1, 4)
            send, recv = send1.at[k, shard], recv1.at[k, shard]
            return remote(quarter, quarter, send, recv, {name1: 1 - own1})
        half = part_of(outs[k], 2 * shard + core, own2, 2)
        send, recv = send2.at[k, shard], recv2.at[k, shard]
        return remote(half, half, send, recv, {name2: 1 - own2})

    def across(k, shard, source=None):
        place = outs[k].at[2 * shard + core]
        return remote(
            place if source is None else source,
            place,
            core_send.at[k, shard],
            core_recv.at[k, shard],
            {"fsdp": partner},
        )

    for k in range(count):
        for step in range(1, depth):
            outward(k, step).start()
        own(k).start()
        across(k, z, ins[k].at[0]).start()

    def arrived(k, shard):
        step = (z + depth - shard) % depth

        @pl.when(shard != z)
        def _():
            inward(k, step).wait_recv()
            joins(k, shard, 0).start()

    def joined(k, shard):
        @pl.when(shard != z)
        def _():
            joins(k, shard, 0).wait_recv()
            joins(k, shard, 1).start()

    def complete(k, shard):
        @pl.when(shard != z)
        def _():
            joins(k, shard, 1).wait_recv()
            across(k, shard).start()

    items = [(k, shard) for k in range(count) for shard in range(depth)]
    lag = 2
    for t in range(len(items) + 2 * lag):
        for late, stage in ((0, arrived), (lag, joined), (2 * lag, complete)):
            if 0 <= t - late < len(items):
                stage(*items[t - late])
    for k in range(count):
        own(k).wait()
        for step in range(1, depth):
            outward(k, step).wait_send()
        for shard in range(depth):
            across(k, shard).wait_send()
            across(k, shard).wait_recv()

            @pl.when(shard != z)
            def _():
                joins(k, shard, 0).wait_send()
                joins(k, shard, 1).wait_send()


def gather_shards(arrays, ways):
    count, depth = len(arrays), ways // 2
    return pl.pallas_call(
        functools.partial(gather_kernel, depth, count),
        out_shape=[jax.ShapeDtypeStruct((ways,) + a.shape, a.dtype) for a in arrays],
        in_specs=[pl.BlockSpec(memory_space=pl.ANY)] * count,
        out_specs=[pl.BlockSpec(memory_space=pltpu.VMEM)] * count,
        scratch_shapes=[pltpu.SemaphoreType.DMA((count,))]
        + [pltpu.SemaphoreType.DMA((count, depth))] * 8,
        compiler_params=pltpu.CompilerParams(
            collective_id=1, has_side_effects=True, vmem_limit_bytes=VMEM_BYTES
        ),
    )(*[a[None] for a in arrays])


def reduce_kernel(depth, count, *refs):
    parts, outs = refs[:count], refs[count : 2 * count]
    rest = refs[2 * count :]
    first, second, third, fourth, held, quarter, joined = [
        rest[i * count : (i + 1) * count] for i in range(7)
    ]
    send0, recv0, send1, recv1, send2, recv2, send3, recv3, send4, recv4 = rest[7 * count :]
    me, x, y = lax.axis_index("fsdp"), lax.axis_index("cp"), lax.axis_index("rep")
    z, core = me // 2, me % 2
    partner = 2 * z + 1 - core
    f32 = jnp.float32

    barrier = pltpu.get_barrier_semaphore()
    others = [{"fsdp": partner}, {"cp": 1 - x}, {"rep": 1 - y}, {"cp": 1 - x, "rep": 1 - y}]
    others += [{"fsdp": 2 * ((z + s) % depth) + core} for s in range(1, depth)]
    for other in others:
        pl.semaphore_signal(barrier, inc=1, device_id=other, device_id_type=MESH_ID)
    pl.semaphore_wait(barrier, len(others))

    def remote(source, place, send, recv, device):
        return pltpu.make_async_remote_copy(
            src_ref=source,
            dst_ref=place,
            send_sem=send,
            recv_sem=recv,
            device_id=device,
            device_id_type=MESH_ID,
        )

    def copy0(k, j):
        return remote(
            parts[k].at[2 * j + 1 - core],
            first[k].at[j],
            send0.at[k, j],
            recv0.at[k, j],
            {"fsdp": partner},
        )

    def axes(j):
        return (x, y, "cp", "rep") if j % 2 == 0 else (y, x, "rep", "cp")

    def copy1(k, j):
        own1, _, name1, _ = axes(j)
        return remote(
            part_of(held[k], j, 1 - own1, 2),
            second[k].at[j],
            send1.at[k, j],
            recv1.at[k, j],
            {name1: 1 - own1},
        )

    def copy2(k, j):
        own1, own2, _, name2 = axes(j)
        return remote(
            part_of(held[k], j, own1 * 2 + 1 - own2, 4),
            third[k].at[j],
            send2.at[k, j],
            recv2.at[k, j],
            {name2: 1 - own2},
        )

    def copy3(k, step):
        to = (z + step) % depth
        return remote(
            quarter[k].at[to],
            fourth[k].at[step],
            send3.at[k, step],
            recv3.at[k, step],
            {"fsdp": 2 * to + core},
        )

    mine = jnp.where(z % 2 == 0, x * 2 + y, y * 2 + x)

    def copy4(k, which):
        place = part_of(joined[k], 0, mine, 4)
        device = [{"cp": 1 - x}, {"rep": 1 - y}, {"cp": 1 - x, "rep": 1 - y}][which]
        return remote(place, place, send4.at[k, which], recv4.at[k, which], device)

    def over_cores(k):
        for j in range(depth):
            copy0(k, j).wait_recv()
            total = parts[k][2 * j + core].astype(f32) + first[k][j].astype(f32)
            held[k][j] = total.astype(held[k].dtype)
            copy1(k, j).start()

    def over_first_axis(k):
        for j in range(depth):
            own1, _, _, _ = axes(j)
            copy1(k, j).wait_recv()
            half = part_of(held[k], j, own1, 2)
            half[...] = (half[...].astype(f32) + second[k][j].astype(f32)).astype(half.dtype)
            copy2(k, j).start()

    def over_second_axis(k):
        for j in range(depth):
            own1, own2, _, _ = axes(j)
            copy2(k, j).wait_recv()
            piece = part_of(held[k], j, own1 * 2 + own2, 4)
            total = piece[...].astype(f32) + third[k][j].astype(f32)
            quarter[k][j] = total.astype(quarter[k].dtype)
        for step in range(1, depth):
            copy3(k, step).start()

    def over_z(k):
        total = quarter[k][z].astype(f32)
        for step in range(1, depth):
            copy3(k, step).wait_recv()
            total = total + fourth[k][step].astype(f32)
        place = part_of(joined[k], 0, mine, 4)
        place[...] = total.astype(place.dtype)
        for which in range(3):
            copy4(k, which).start()

    def finish(k):
        for which in range(3):
            copy4(k, which).wait_recv()
        outs[k][...] = joined[k][0].astype(f32)

    for k in range(count):
        for j in range(depth):
            copy0(k, j).start()
    stages = (over_cores, over_first_axis, over_second_axis, over_z, finish)
    for t in range(count + len(stages) - 1):
        for late, stage in enumerate(stages):
            if 0 <= t - late < count:
                stage(t - late)
    for k in range(count):
        for j in range(depth):
            copy0(k, j).wait_send()
            copy1(k, j).wait_send()
            copy2(k, j).wait_send()
        for step in range(1, depth):
            copy3(k, step).wait_send()
        for which in range(3):
            copy4(k, which).wait_send()


def reduce_shards(arrays):
    count, ways = len(arrays), arrays[0].shape[0]
    depth = ways // 2
    kind = arrays[0].dtype
    wholes = [(depth,) + a.shape[1:] for a in arrays]
    halves, quarters = [], []
    for a in arrays:
        rows, columns = a.shape[1:]
        by_columns = columns % (4 * 128) == 0
        halves.append((depth, rows, columns // 2) if by_columns else (depth, rows // 2, columns))
        quarters.append((depth, rows, columns // 4) if by_columns else (depth, rows // 4, columns))
    buffers = []
    for shapes in (wholes, halves, quarters, quarters, wholes, quarters):
        buffers += [pltpu.VMEM(s, kind) for s in shapes]
    buffers += [pltpu.VMEM((1,) + a.shape[1:], kind) for a in arrays]
    sems = [pltpu.SemaphoreType.DMA((count, depth))] * 8 + [pltpu.SemaphoreType.DMA((count, 3))] * 2
    return pl.pallas_call(
        functools.partial(reduce_kernel, depth, count),
        out_shape=[jax.ShapeDtypeStruct(a.shape[1:], jnp.float32) for a in arrays],
        in_specs=[pl.BlockSpec(memory_space=pltpu.VMEM)] * count,
        out_specs=[pl.BlockSpec(memory_space=pltpu.VMEM)] * count,
        scratch_shapes=buffers + sems,
        compiler_params=pltpu.CompilerParams(
            collective_id=2, has_side_effects=True, vmem_limit_bytes=VMEM_BYTES
        ),
    )(*arrays)


def rope_tables(positions):
    half = HEAD_SIZE // 2
    freq = THETA ** (-2.0 * jnp.arange(half, dtype=jnp.float32) / HEAD_SIZE)
    angle = positions.astype(jnp.float32)[:, None] * freq[None, :]
    return (jnp.cos(angle), jnp.sin(angle))


def apply_rotation(tensor, cosine_table, sine_table, direction):
    half = HEAD_SIZE // 2
    first = tensor[..., :half]
    second = tensor[..., half:]
    cos_b = cosine_table[:, None, :]
    sin_b = sine_table[:, None, :] * direction
    return jnp.concatenate(
        [first * cos_b - second * sin_b, first * sin_b + second * cos_b], axis=-1
    )


def doc_positions(seg_row):
    index_row = jnp.arange(seg_row.shape[0], dtype=jnp.int32)
    starts = jnp.sum((seg_row[None, :] < seg_row[:, None]).astype(jnp.int32), axis=1)
    return index_row - starts


def times_transposed(left, right):
    return lax.dot_general(
        left, right, (((1,), (1,)), ((), ())), preferred_element_type=jnp.float32
    )


def transposed_times(left, right):
    return lax.dot_general(
        left, right, (((0,), (0,)), ((), ())), preferred_element_type=jnp.float32
    )


def norm_forward(values, gain):
    inv_rms = lax.rsqrt(jnp.mean(values * values, axis=-1, keepdims=True) + EPS)
    normed = values * inv_rms
    return (normed, inv_rms, (normed * gain.astype(jnp.float32)).astype(jnp.bfloat16))


def norm_backward(d_normed, normed, inv_rms, gain):
    gain_grad = jnp.sum(d_normed * normed, axis=0)
    scaled = d_normed * gain.astype(jnp.float32)
    return (
        gain_grad,
        inv_rms * (scaled - normed * jnp.mean(scaled * normed, axis=-1, keepdims=True)),
    )


def score_block(query_rows, keys_three_axis, visible):
    row_span = query_rows.shape[0]
    grouped_heads = query_rows.reshape(
        row_span, KEY_VALUE_HEADS, QUERY_HEADS // KEY_VALUE_HEADS, HEAD_SIZE
    )
    scores = jnp.einsum(
        "nkgd,mkd->kgnm", grouped_heads, keys_three_axis, preferred_element_type=jnp.float32
    ) * HEAD_SIZE ** (-0.5)
    return jnp.where(visible[None, None], scores, MASKED)


def attend(query_rows, keys_three_axis, values_three_axis, visible):
    row_span = query_rows.shape[0]
    scores = score_block(query_rows, keys_three_axis, visible)
    top = jnp.max(scores, axis=-1, keepdims=True)
    expo = jnp.exp(scores - top)
    total = jnp.sum(expo, axis=-1, keepdims=True)
    probs = (expo / total).astype(jnp.bfloat16)
    log_total = top + jnp.log(total)
    mixed_heads = jnp.einsum(
        "kgnm,mkd->nkgd", probs, values_three_axis, preferred_element_type=jnp.float32
    )
    return (mixed_heads.reshape(row_span, QUERY_HEADS * HEAD_SIZE).astype(jnp.bfloat16), log_total)


def attend_back(
    mixed_gradient, mixed_heads, query_rows, keys_three_axis, values_three_axis, visible, log_total
):
    row_span = query_rows.shape[0]
    query_group = QUERY_HEADS // KEY_VALUE_HEADS
    scores = score_block(query_rows, keys_three_axis, visible)
    probs = jnp.exp(scores - log_total)
    probs_b = probs.astype(jnp.bfloat16)
    grouped_gradient = mixed_gradient.reshape(row_span, KEY_VALUE_HEADS, query_group, HEAD_SIZE)
    d_values = jnp.einsum(
        "kgnm,nkgd->mkd", probs_b, grouped_gradient, preferred_element_type=jnp.float32
    )
    d_probs = jnp.einsum(
        "nkgd,mkd->kgnm", grouped_gradient, values_three_axis, preferred_element_type=jnp.float32
    )
    change_amount = jnp.sum(
        grouped_gradient.astype(jnp.float32)
        * mixed_heads.reshape(row_span, KEY_VALUE_HEADS, query_group, HEAD_SIZE).astype(
            jnp.float32
        ),
        axis=-1,
    )
    change_amount = jnp.transpose(change_amount, (1, 2, 0))[..., None]
    d_scores = (probs * (d_probs - change_amount)).astype(jnp.bfloat16)
    grouped_heads = query_rows.reshape(row_span, KEY_VALUE_HEADS, query_group, HEAD_SIZE)
    d_queries = jnp.einsum(
        "kgnm,mkd->nkgd", d_scores, keys_three_axis, preferred_element_type=jnp.float32
    ) * HEAD_SIZE ** (-0.5)
    d_keys = jnp.einsum(
        "kgnm,nkgd->mkd", d_scores, grouped_heads, preferred_element_type=jnp.float32
    ) * HEAD_SIZE ** (-0.5)
    return (d_queries.reshape(row_span, QUERY_HEADS, HEAD_SIZE), d_keys, d_values)


def swap_halves(value):
    return lax.ppermute(value, "cp", [(0, 1), (1, 0)])


def both_halves(value, axis):
    other = swap_halves(value)
    first = lax.axis_index("cp") == 0
    return jnp.concatenate(
        [jnp.where(first, value, other), jnp.where(first, other, value)], axis=axis
    )


def shards(
    ways, copies, block_input, segment_ids, attn_gain, w_qkv, w_out, mlp_gain, w_gate, w_up, w_down, out_cotangent
):
    residual = block_input[0].astype(jnp.float32)
    row_span = residual.shape[0]
    query_columns = QUERY_HEADS * HEAD_SIZE
    key_columns = KEY_VALUE_HEADS * HEAD_SIZE
    shard = attn_gain.shape[0]
    gains = jnp.zeros((16, 512), jnp.bfloat16)
    gains = gains.at[0, :shard].set(attn_gain).at[1, :shard].set(mlp_gain)
    own_weights = [jnp.concatenate([w_qkv, w_out], axis=1), gains, w_gate, w_up, w_down]
    if copies == (2, 2):
        gathered = gather_shards(own_weights, ways)
    else:
        gathered = [lax.all_gather(w, "fsdp") for w in own_weights]
    both_full, gate_full, up_full, down_full = [
        gathered[i].reshape(-1, gathered[i].shape[-1]) for i in (0, 2, 3, 4)
    ]
    qkv_full, out_full = both_full[:, : w_qkv.shape[1]], both_full[:, w_qkv.shape[1] :]
    gain_a = gathered[1][:, 0, :shard].reshape(-1)
    gain_m = gathered[1][:, 1, :shard].reshape(-1)
    whole_ids = both_halves(segment_ids, 1)[0]
    every_length = whole_ids.shape[0]
    offset = lax.axis_index("cp") * row_span
    key_index = jnp.arange(every_length, dtype=jnp.int32)
    key_positions = doc_positions(whole_ids)
    query_index = offset + jnp.arange(row_span, dtype=jnp.int32)
    query_positions = lax.dynamic_slice_in_dim(key_positions, offset, row_span)
    local_ids = segment_ids[0]
    visible = (whole_ids[None, :] == local_ids[:, None]) & (
        key_index[None, :] <= query_index[:, None]
    )
    query_cosine, query_sine = rope_tables(query_positions)
    k_cos, k_sin = rope_tables(key_positions)
    normed1, inv_rms1, xn = norm_forward(residual, gain_a)
    output_projection = jnp.dot(xn, qkv_full, preferred_element_type=jnp.float32)
    query_rows = apply_rotation(
        output_projection[:, :query_columns].reshape(row_span, QUERY_HEADS, HEAD_SIZE),
        query_cosine,
        query_sine,
        1.0,
    ).astype(jnp.bfloat16)
    keys_local = (
        apply_rotation(
            output_projection[:, query_columns : query_columns + key_columns].reshape(
                row_span, KEY_VALUE_HEADS, HEAD_SIZE
            ),
            query_cosine,
            query_sine,
            1.0,
        )
        .astype(jnp.bfloat16)
        .reshape(row_span, key_columns)
    )
    values_local = output_projection[:, query_columns + key_columns :].astype(jnp.bfloat16)
    every_pair = both_halves(jnp.concatenate([keys_local, values_local], axis=1), 0)
    every_key, every_value = every_pair[:, :key_columns], every_pair[:, key_columns:]
    keys_three_axis = every_key.reshape(every_length, KEY_VALUE_HEADS, HEAD_SIZE)
    values_three_axis = every_value.reshape(every_length, KEY_VALUE_HEADS, HEAD_SIZE)
    attn_mix, log_total = attend(query_rows, keys_three_axis, values_three_axis, visible)
    mid = residual + jnp.dot(attn_mix, out_full, preferred_element_type=jnp.float32)
    normed2, inv_rms2, hidden_n = norm_forward(mid, gain_m)
    gate = jnp.dot(hidden_n, gate_full, preferred_element_type=jnp.float32)
    up_val = jnp.dot(hidden_n, up_full, preferred_element_type=jnp.float32)
    sigma = jax.nn.sigmoid(gate)
    silu_gate = gate * sigma
    act = (silu_gate * up_val).astype(jnp.bfloat16)
    block_output = (mid + jnp.dot(act, down_full, preferred_element_type=jnp.float32)).astype(
        jnp.bfloat16
    )
    cotangent = out_cotangent[0]
    d_act = times_transposed(cotangent, down_full)
    down_grad = transposed_times(act, cotangent)
    d_gate = (d_act * up_val * sigma * (1.0 + gate * (1.0 - sigma))).astype(jnp.bfloat16)
    d_up = (d_act * silu_gate).astype(jnp.bfloat16)
    gate_grad = transposed_times(hidden_n, d_gate)
    up_grad = transposed_times(hidden_n, d_up)
    d_hn = times_transposed(d_gate, gate_full) + times_transposed(d_up, up_full)
    mlp_gain_grad, d_norm2 = norm_backward(d_hn, normed2, inv_rms2, gain_m)
    d_mid = cotangent.astype(jnp.float32) + d_norm2
    d_mid_b = d_mid.astype(jnp.bfloat16)
    out_grad = transposed_times(attn_mix, d_mid_b)
    d_attn = times_transposed(d_mid_b, out_full).astype(jnp.bfloat16)
    d_queries, d_keys, d_values = attend_back(
        d_attn, attn_mix, query_rows, keys_three_axis, values_three_axis, visible, log_total
    )
    d_keys_flat = apply_rotation(d_keys, k_cos, k_sin, -1.0).reshape(every_length, key_columns)
    d_values_flat = d_values.reshape(every_length, key_columns)
    pair = jnp.concatenate([d_keys_flat, d_values_flat], axis=1)
    away = lax.dynamic_slice_in_dim(pair, row_span - offset, row_span)
    pair_part = lax.dynamic_slice_in_dim(pair, offset, row_span) + swap_halves(
        away.astype(jnp.bfloat16)
    ).astype(jnp.float32)
    d_proj = jnp.concatenate(
        [
            apply_rotation(d_queries, query_cosine, query_sine, -1.0).reshape(
                row_span, query_columns
            ),
            pair_part,
        ],
        axis=1,
    ).astype(jnp.bfloat16)
    qkv_grad = transposed_times(xn, d_proj)
    d_xn = times_transposed(d_proj, qkv_full)
    attn_gain_grad, d_norm1 = norm_backward(d_xn, normed1, inv_rms1, gain_a)
    input_grad = d_mid + d_norm1
    if copies == (2, 2):
        bf16 = jnp.bfloat16
        gain_grads = jnp.stack(
            [attn_gain_grad.reshape(ways, shard), mlp_gain_grad.reshape(ways, shard)], axis=1
        )
        gain_grads = jnp.pad(gain_grads, ((0, 0), (0, 14), (0, 512 - shard))).astype(bf16)
        both = jnp.concatenate([qkv_grad.astype(bf16), out_grad.astype(bf16)], axis=1)
        stacked = [
            g.astype(bf16).reshape(ways, -1, g.shape[-1])
            for g in (gate_grad, up_grad, down_grad, both)
        ]
        gain_s, gate_s, up_s, down_s, both_s = reduce_shards([gain_grads] + stacked)
        qkv_s, out_s = both_s[:, : w_qkv.shape[1]], both_s[:, w_qkv.shape[1] :]
        gain_a_s, gain_m_s = gain_s[0, :shard], gain_s[1, :shard]
    else:
        grads = (attn_gain_grad, qkv_grad, out_grad, mlp_gain_grad, gate_grad, up_grad, down_grad)
        grads = [lax.psum_scatter(g, "fsdp", scatter_dimension=0, tiled=True) for g in grads]
        gain_a_s, qkv_s, out_s, gain_m_s, gate_s, up_s, down_s = lax.psum(grads, ("rep", "cp"))
    return (
        block_output[None],
        input_grad[None],
        gain_a_s,
        qkv_s,
        out_s,
        gain_m_s,
        gate_s,
        up_s,
        down_s,
    )


def solution(mesh):
    ways = mesh.shape["fsdp"]
    copies = (mesh.shape["rep"], mesh.shape["cp"])
    return jax.shard_map(
        functools.partial(shards, ways, copies),
        mesh=mesh,
        in_specs=(
            P(("fsdp", "rep"), "cp", None),
            P(("fsdp", "rep"), "cp"),
            P("fsdp"),
            P("fsdp", None),
            P("fsdp", None),
            P("fsdp"),
            P("fsdp", None),
            P("fsdp", None),
            P("fsdp", None),
            P(("fsdp", "rep"), "cp", None),
        ),
        out_specs=(
            P(("fsdp", "rep"), "cp", None),
            P(("fsdp", "rep"), "cp", None),
            P("fsdp"),
            P("fsdp", None),
            P("fsdp", None),
            P("fsdp"),
            P("fsdp", None),
            P("fsdp", None),
            P("fsdp", None),
        ),
        check_vma=False,
    )
```

```python
import functools

import jax
import jax.numpy as jnp
from jax import lax
from jax.experimental import pallas as pl
from jax.experimental.pallas import tpu as pltpu
from jax.sharding import PartitionSpec as P

QUERY_HEADS = 9
KEY_VALUE_HEADS = 3
HEAD_SIZE = 64


EPS = 1e-05
THETA = 100000.0
MASKED = -1e30

VMEM_BYTES = 50 * 1024 * 1024
MESH_ID = pl.DeviceIdType.MESH


def part_of(ref, lead, index, parts):
    rows, columns = ref.shape[-2:]
    if columns % (4 * 128) == 0:
        size = columns // parts
        return ref.at[lead, :, pl.ds(pl.multiple_of(index * size, size), size)]
    size = rows // parts
    return ref.at[lead, pl.ds(pl.multiple_of(index * size, size), size), :]


def gather_kernel(depth, count, *refs):
    ins, outs = refs[:count], refs[count : 2 * count]
    own_sem, z_send, z_recv, send1, recv1, send2, recv2, core_send, core_recv = refs[2 * count :]
    me, x, y = lax.axis_index("fsdp"), lax.axis_index("cp"), lax.axis_index("rep")
    z, core = me // 2, me % 2
    partner = 2 * z + 1 - core
    barrier = pltpu.get_barrier_semaphore()
    others = [{"fsdp": partner}, {"cp": 1 - x}, {"rep": 1 - y}]
    others += [{"fsdp": 2 * ((z + s) % depth) + core} for s in range(1, depth)]
    for other in others:
        pl.semaphore_signal(barrier, inc=1, device_id=other, device_id_type=MESH_ID)
    pl.semaphore_wait(barrier, len(others))

    def remote(source, place, send, recv, device):
        return pltpu.make_async_remote_copy(
            src_ref=source,
            dst_ref=place,
            send_sem=send,
            recv_sem=recv,
            device_id=device,
            device_id_type=MESH_ID,
        )

    def axes(j):
        return (x, y, "cp", "rep") if j % 2 == 0 else (y, x, "rep", "cp")

    def own(k):
        return pltpu.make_async_copy(ins[k].at[0], outs[k].at[me], own_sem.at[k])

    def outward(k, step):
        mine = jnp.where(z % 2 == 0, y * 2 + x, x * 2 + y)
        return remote(
            part_of(ins[k], 0, mine, 4),
            part_of(outs[k], me, mine, 4),
            z_send.at[k, step],
            z_recv.at[k, step],
            {"fsdp": 2 * ((z + step) % depth) + core},
        )

    def inward(k, step):
        shard = (z + depth - step) % depth
        even = shard % 2 == 0
        mine = jnp.where(even, y * 2 + x, x * 2 + y)
        place = part_of(outs[k], 2 * shard + core, mine, 4)
        return remote(place, place, z_send.at[k, step], z_recv.at[k, step], {"fsdp": partner})

    def joins(k, shard, which):
        own1, own2, name1, name2 = axes(shard)
        if which == 0:
            quarter = part_of(outs[k], 2 * shard + core, own2 * 2 + own1, 4)
            send, recv = send1.at[k, shard], recv1.at[k, shard]
            return remote(quarter, quarter, send, recv, {name1: 1 - own1})
        half = part_of(outs[k], 2 * shard + core, own2, 2)
        send, recv = send2.at[k, shard], recv2.at[k, shard]
        return remote(half, half, send, recv, {name2: 1 - own2})

    def across(k, shard, source=None):
        place = outs[k].at[2 * shard + core]
        return remote(
            place if source is None else source,
            place,
            core_send.at[k, shard],
            core_recv.at[k, shard],
            {"fsdp": partner},
        )

    for k in range(count):
        for step in range(1, depth):
            outward(k, step).start()
        own(k).start()
        across(k, z, ins[k].at[0]).start()

    def arrived(k, shard):
        step = (z + depth - shard) % depth

        @pl.when(shard != z)
        def _():
            inward(k, step).wait_recv()
            joins(k, shard, 0).start()

    def joined(k, shard):
        @pl.when(shard != z)
        def _():
            joins(k, shard, 0).wait_recv()
            joins(k, shard, 1).start()

    def complete(k, shard):
        @pl.when(shard != z)
        def _():
            joins(k, shard, 1).wait_recv()
            across(k, shard).start()

    items = [(k, shard) for k in range(count) for shard in range(depth)]
    lag = 2
    for t in range(len(items) + 2 * lag):
        for late, stage in ((0, arrived), (lag, joined), (2 * lag, complete)):
            if 0 <= t - late < len(items):
                stage(*items[t - late])
    for k in range(count):
        own(k).wait()
        for step in range(1, depth):
            outward(k, step).wait_send()
        for shard in range(depth):
            across(k, shard).wait_send()
            across(k, shard).wait_recv()

            @pl.when(shard != z)
            def _():
                joins(k, shard, 0).wait_send()
                joins(k, shard, 1).wait_send()


def gather_shards(arrays, ways):
    count, depth = len(arrays), ways // 2
    return pl.pallas_call(
        functools.partial(gather_kernel, depth, count),
        out_shape=[jax.ShapeDtypeStruct((ways,) + a.shape, a.dtype) for a in arrays],
        in_specs=[pl.BlockSpec(memory_space=pl.ANY)] * count,
        out_specs=[pl.BlockSpec(memory_space=pltpu.VMEM)] * count,
        scratch_shapes=[pltpu.SemaphoreType.DMA((count,))]
        + [pltpu.SemaphoreType.DMA((count, depth))] * 8,
        compiler_params=pltpu.CompilerParams(
            collective_id=1, has_side_effects=True, vmem_limit_bytes=VMEM_BYTES
        ),
    )(*[a[None] for a in arrays])


def reduce_kernel(depth, count, *refs):
    gains, factors, rest = refs[0], refs[1 : 2 * count - 1], refs[2 * count - 1 :]
    outs, products, rest = rest[:count], rest[count : 2 * count - 1], rest[2 * count - 1 :]
    parts = (gains,) + tuple(products)
    first, second, third, fourth, held, quarter, joined = [
        rest[i * count : (i + 1) * count] for i in range(7)
    ]
    send0, recv0, send1, recv1, send2, recv2, send3, recv3, send4, recv4 = rest[7 * count :]
    me, x, y = lax.axis_index("fsdp"), lax.axis_index("cp"), lax.axis_index("rep")
    z, core = me // 2, me % 2
    partner = 2 * z + 1 - core
    f32 = jnp.float32

    barrier = pltpu.get_barrier_semaphore()
    others = [{"fsdp": partner}, {"cp": 1 - x}, {"rep": 1 - y}, {"cp": 1 - x, "rep": 1 - y}]
    others += [{"fsdp": 2 * ((z + s) % depth) + core} for s in range(1, depth)]
    for other in others:
        pl.semaphore_signal(barrier, inc=1, device_id=other, device_id_type=MESH_ID)
    pl.semaphore_wait(barrier, len(others))

    def remote(source, place, send, recv, device):
        return pltpu.make_async_remote_copy(
            src_ref=source,
            dst_ref=place,
            send_sem=send,
            recv_sem=recv,
            device_id=device,
            device_id_type=MESH_ID,
        )

    def copy0(k, j):
        return remote(
            parts[k].at[2 * j + 1 - core],
            first[k].at[j],
            send0.at[k, j],
            recv0.at[k, j],
            {"fsdp": partner},
        )

    def axes(j):
        return (x, y, "cp", "rep") if j % 2 == 0 else (y, x, "rep", "cp")

    def copy1(k, j):
        own1, _, name1, _ = axes(j)
        return remote(
            part_of(held[k], j, 1 - own1, 2),
            second[k].at[j],
            send1.at[k, j],
            recv1.at[k, j],
            {name1: 1 - own1},
        )

    def copy2(k, j):
        own1, own2, _, name2 = axes(j)
        return remote(
            part_of(held[k], j, own1 * 2 + 1 - own2, 4),
            third[k].at[j],
            send2.at[k, j],
            recv2.at[k, j],
            {name2: 1 - own2},
        )

    def copy3(k, step):
        to = (z + step) % depth
        return remote(
            quarter[k].at[to],
            fourth[k].at[step],
            send3.at[k, step],
            recv3.at[k, step],
            {"fsdp": 2 * to + core},
        )

    mine = jnp.where(z % 2 == 0, x * 2 + y, y * 2 + x)

    def copy4(k, which):
        place = part_of(joined[k], 0, mine, 4)
        device = [{"cp": 1 - x}, {"rep": 1 - y}, {"cp": 1 - x, "rep": 1 - y}][which]
        return remote(place, place, send4.at[k, which], recv4.at[k, which], device)

    def multiply(k):
        if k > 0:
            left, right = factors[2 * k - 2], factors[2 * k - 1]
            ways, rows, columns = parts[k].shape
            contract = (((0,), (0,)), ((), ()))
            if columns % 512 == 0:

                def some_columns(n, carry):
                    span = pl.ds(pl.multiple_of(n * 512, 512), 512)
                    product = lax.dot_general(
                        left[...], right[:, span], contract, preferred_element_type=f32
                    )
                    for i in range(ways):
                        block = product[i * rows : (i + 1) * rows]
                        parts[k][i, :, span] = block.astype(parts[k].dtype)
                    return carry

                lax.fori_loop(0, columns // 512, some_columns, 0)
            else:

                def some_rows(n, carry):
                    span = pl.ds(pl.multiple_of(n * 2 * rows, 2 * rows), 2 * rows)
                    product = lax.dot_general(
                        left[:, span], right[...], contract, preferred_element_type=f32
                    )
                    for i in range(2):
                        block = product[i * rows : (i + 1) * rows]
                        parts[k][2 * n + i] = block.astype(parts[k].dtype)
                    return carry

                lax.fori_loop(0, ways // 2, some_rows, 0)
        for j in range(depth):
            copy0(k, j).start()

    def over_cores(k):
        for j in range(depth):
            copy0(k, j).wait_recv()
            total = parts[k][2 * j + core].astype(f32) + first[k][j].astype(f32)
            held[k][j] = total.astype(held[k].dtype)
            copy1(k, j).start()

    def over_first_axis(k):
        for j in range(depth):
            own1, _, _, _ = axes(j)
            copy1(k, j).wait_recv()
            half = part_of(held[k], j, own1, 2)
            half[...] = (half[...].astype(f32) + second[k][j].astype(f32)).astype(half.dtype)
            copy2(k, j).start()

    def over_second_axis(k):
        for j in range(depth):
            own1, own2, _, _ = axes(j)
            copy2(k, j).wait_recv()
            piece = part_of(held[k], j, own1 * 2 + own2, 4)
            total = piece[...].astype(f32) + third[k][j].astype(f32)
            quarter[k][j] = total.astype(quarter[k].dtype)
        for step in range(1, depth):
            copy3(k, step).start()

    def over_z(k):
        total = quarter[k][z].astype(f32)
        for step in range(1, depth):
            copy3(k, step).wait_recv()
            total = total + fourth[k][step].astype(f32)
        place = part_of(joined[k], 0, mine, 4)
        place[...] = total.astype(place.dtype)
        for which in range(3):
            copy4(k, which).start()

    def finish(k):
        for which in range(3):
            copy4(k, which).wait_recv()
        outs[k][...] = joined[k][0].astype(f32)

    stages = (multiply, over_cores, over_first_axis, over_second_axis, over_z, finish)
    for t in range(count + len(stages) - 1):
        for late, stage in enumerate(stages):
            if 0 <= t - late < count:
                stage(t - late)
    for k in range(count):
        for j in range(depth):
            copy0(k, j).wait_send()
            copy1(k, j).wait_send()
            copy2(k, j).wait_send()
        for step in range(1, depth):
            copy3(k, step).wait_send()
        for which in range(3):
            copy4(k, which).wait_send()


def reduce_shards(gains, factors):
    ways = gains.shape[0]
    depth, kind = ways // 2, gains.dtype
    arrays = [gains] + [
        jax.ShapeDtypeStruct((ways, left.shape[1] // ways, right.shape[1]), kind)
        for left, right in factors
    ]
    count = len(arrays)
    operands = [gains] + [f for pair in factors for f in pair]
    wholes = [(depth,) + a.shape[1:] for a in arrays]
    halves, quarters = [], []
    for a in arrays:
        rows, columns = a.shape[1:]
        by_columns = columns % (4 * 128) == 0
        halves.append((depth, rows, columns // 2) if by_columns else (depth, rows // 2, columns))
        quarters.append((depth, rows, columns // 4) if by_columns else (depth, rows // 4, columns))
    buffers = [pltpu.VMEM(a.shape, kind) for a in arrays[1:]]
    for shapes in (wholes, halves, quarters, quarters, wholes, quarters):
        buffers += [pltpu.VMEM(s, kind) for s in shapes]
    buffers += [pltpu.VMEM((1,) + a.shape[1:], kind) for a in arrays]
    sems = [pltpu.SemaphoreType.DMA((count, depth))] * 8 + [pltpu.SemaphoreType.DMA((count, 3))] * 2
    return pl.pallas_call(
        functools.partial(reduce_kernel, depth, count),
        out_shape=[jax.ShapeDtypeStruct(a.shape[1:], jnp.float32) for a in arrays],
        in_specs=[pl.BlockSpec(memory_space=pltpu.VMEM)] * len(operands),
        out_specs=[pl.BlockSpec(memory_space=pltpu.VMEM)] * count,
        scratch_shapes=buffers + sems,
        compiler_params=pltpu.CompilerParams(
            collective_id=2, has_side_effects=True, vmem_limit_bytes=VMEM_BYTES
        ),
    )(*operands)


def rope_tables(positions):
    half = HEAD_SIZE // 2
    freq = THETA ** (-2.0 * jnp.arange(half, dtype=jnp.float32) / HEAD_SIZE)
    angle = positions.astype(jnp.float32)[:, None] * freq[None, :]
    return (jnp.cos(angle), jnp.sin(angle))


def apply_rotation(tensor, cosine_table, sine_table, direction):
    half = HEAD_SIZE // 2
    first = tensor[..., :half]
    second = tensor[..., half:]
    cos_b = cosine_table[:, None, :]
    sin_b = sine_table[:, None, :] * direction
    return jnp.concatenate(
        [first * cos_b - second * sin_b, first * sin_b + second * cos_b], axis=-1
    )


def doc_positions(seg_row):
    index_row = jnp.arange(seg_row.shape[0], dtype=jnp.int32)
    starts = jnp.sum((seg_row[None, :] < seg_row[:, None]).astype(jnp.int32), axis=1)
    return index_row - starts


def times_transposed(left, right):
    return lax.dot_general(
        left, right, (((1,), (1,)), ((), ())), preferred_element_type=jnp.float32
    )


def transposed_times(left, right):
    return lax.dot_general(
        left, right, (((0,), (0,)), ((), ())), preferred_element_type=jnp.float32
    )


def norm_forward(values, gain):
    inv_rms = lax.rsqrt(jnp.mean(values * values, axis=-1, keepdims=True) + EPS)
    normed = values * inv_rms
    return (normed, inv_rms, (normed * gain.astype(jnp.float32)).astype(jnp.bfloat16))


def norm_backward(d_normed, normed, inv_rms, gain):
    gain_grad = jnp.sum(d_normed * normed, axis=0)
    scaled = d_normed * gain.astype(jnp.float32)
    return (
        gain_grad,
        inv_rms * (scaled - normed * jnp.mean(scaled * normed, axis=-1, keepdims=True)),
    )


def score_block(query_rows, keys_three_axis, visible):
    row_span = query_rows.shape[0]
    grouped_heads = query_rows.reshape(
        row_span, KEY_VALUE_HEADS, QUERY_HEADS // KEY_VALUE_HEADS, HEAD_SIZE
    )
    scores = jnp.einsum(
        "nkgd,mkd->kgnm", grouped_heads, keys_three_axis, preferred_element_type=jnp.float32
    ) * HEAD_SIZE ** (-0.5)
    return jnp.where(visible[None, None], scores, MASKED)


def attend(query_rows, keys_three_axis, values_three_axis, visible):
    row_span = query_rows.shape[0]
    scores = score_block(query_rows, keys_three_axis, visible)
    top = jnp.max(scores, axis=-1, keepdims=True)
    expo = jnp.exp(scores - top)
    total = jnp.sum(expo, axis=-1, keepdims=True)
    probs = (expo / total).astype(jnp.bfloat16)
    log_total = top + jnp.log(total)
    mixed_heads = jnp.einsum(
        "kgnm,mkd->nkgd", probs, values_three_axis, preferred_element_type=jnp.float32
    )
    return (mixed_heads.reshape(row_span, QUERY_HEADS * HEAD_SIZE).astype(jnp.bfloat16), log_total)


def attend_back(
    mixed_gradient, mixed_heads, query_rows, keys_three_axis, values_three_axis, visible, log_total
):
    row_span = query_rows.shape[0]
    query_group = QUERY_HEADS // KEY_VALUE_HEADS
    scores = score_block(query_rows, keys_three_axis, visible)
    probs = jnp.exp(scores - log_total)
    probs_b = probs.astype(jnp.bfloat16)
    grouped_gradient = mixed_gradient.reshape(row_span, KEY_VALUE_HEADS, query_group, HEAD_SIZE)
    d_values = jnp.einsum(
        "kgnm,nkgd->mkd", probs_b, grouped_gradient, preferred_element_type=jnp.float32
    )
    d_probs = jnp.einsum(
        "nkgd,mkd->kgnm", grouped_gradient, values_three_axis, preferred_element_type=jnp.float32
    )
    change_amount = jnp.sum(
        grouped_gradient.astype(jnp.float32)
        * mixed_heads.reshape(row_span, KEY_VALUE_HEADS, query_group, HEAD_SIZE).astype(
            jnp.float32
        ),
        axis=-1,
    )
    change_amount = jnp.transpose(change_amount, (1, 2, 0))[..., None]
    d_scores = (probs * (d_probs - change_amount)).astype(jnp.bfloat16)
    grouped_heads = query_rows.reshape(row_span, KEY_VALUE_HEADS, query_group, HEAD_SIZE)
    d_queries = jnp.einsum(
        "kgnm,mkd->nkgd", d_scores, keys_three_axis, preferred_element_type=jnp.float32
    ) * HEAD_SIZE ** (-0.5)
    d_keys = jnp.einsum(
        "kgnm,nkgd->mkd", d_scores, grouped_heads, preferred_element_type=jnp.float32
    ) * HEAD_SIZE ** (-0.5)
    return (d_queries.reshape(row_span, QUERY_HEADS, HEAD_SIZE), d_keys, d_values)


def swap_halves(value):
    return lax.ppermute(value, "cp", [(0, 1), (1, 0)])


def both_halves(value, axis):
    other = swap_halves(value)
    first = lax.axis_index("cp") == 0
    return jnp.concatenate(
        [jnp.where(first, value, other), jnp.where(first, other, value)], axis=axis
    )


def shards(
    ways, copies, block_input, segment_ids, attn_gain, w_qkv, w_out, mlp_gain, w_gate, w_up, w_down, out_cotangent
):
    residual = block_input[0].astype(jnp.float32)
    row_span = residual.shape[0]
    query_columns = QUERY_HEADS * HEAD_SIZE
    key_columns = KEY_VALUE_HEADS * HEAD_SIZE
    shard = attn_gain.shape[0]
    gains = jnp.zeros((16, 512), jnp.bfloat16)
    gains = gains.at[0, :shard].set(attn_gain).at[1, :shard].set(mlp_gain)
    own_weights = [jnp.concatenate([w_qkv, w_out], axis=1), gains, w_gate, w_up, w_down]
    if copies == (2, 2):
        gathered = gather_shards(own_weights, ways)
    else:
        gathered = [lax.all_gather(w, "fsdp") for w in own_weights]
    both_full, gate_full, up_full, down_full = [
        gathered[i].reshape(-1, gathered[i].shape[-1]) for i in (0, 2, 3, 4)
    ]
    qkv_full, out_full = both_full[:, : w_qkv.shape[1]], both_full[:, w_qkv.shape[1] :]
    gain_a = gathered[1][:, 0, :shard].reshape(-1)
    gain_m = gathered[1][:, 1, :shard].reshape(-1)
    whole_ids = both_halves(segment_ids, 1)[0]
    every_length = whole_ids.shape[0]
    offset = lax.axis_index("cp") * row_span
    key_index = jnp.arange(every_length, dtype=jnp.int32)
    key_positions = doc_positions(whole_ids)
    query_index = offset + jnp.arange(row_span, dtype=jnp.int32)
    query_positions = lax.dynamic_slice_in_dim(key_positions, offset, row_span)
    local_ids = segment_ids[0]
    visible = (whole_ids[None, :] == local_ids[:, None]) & (
        key_index[None, :] <= query_index[:, None]
    )
    query_cosine, query_sine = rope_tables(query_positions)
    k_cos, k_sin = rope_tables(key_positions)
    normed1, inv_rms1, xn = norm_forward(residual, gain_a)
    key_projection = jnp.dot(xn, qkv_full[:, query_columns:], preferred_element_type=jnp.float32)
    query_projection = jnp.dot(xn, qkv_full[:, :query_columns], preferred_element_type=jnp.float32)
    query_rows = apply_rotation(
        query_projection.reshape(row_span, QUERY_HEADS, HEAD_SIZE),
        query_cosine,
        query_sine,
        1.0,
    ).astype(jnp.bfloat16)
    keys_local = (
        apply_rotation(
            key_projection[:, :key_columns].reshape(
                row_span, KEY_VALUE_HEADS, HEAD_SIZE
            ),
            query_cosine,
            query_sine,
            1.0,
        )
        .astype(jnp.bfloat16)
        .reshape(row_span, key_columns)
    )
    values_local = key_projection[:, key_columns:].astype(jnp.bfloat16)
    pair_local = jnp.concatenate([keys_local, values_local], axis=1)
    pair_other = swap_halves(pair_local)
    d_act = times_transposed(out_cotangent[0], down_full)
    pair_other, query_rows, d_act = lax.optimization_barrier((pair_other, query_rows, d_act))
    first = lax.axis_index("cp") == 0
    every_pair = jnp.concatenate(
        [jnp.where(first, pair_local, pair_other), jnp.where(first, pair_other, pair_local)], axis=0
    )
    every_key, every_value = every_pair[:, :key_columns], every_pair[:, key_columns:]
    keys_three_axis = every_key.reshape(every_length, KEY_VALUE_HEADS, HEAD_SIZE)
    values_three_axis = every_value.reshape(every_length, KEY_VALUE_HEADS, HEAD_SIZE)
    attn_mix, log_total = attend(query_rows, keys_three_axis, values_three_axis, visible)
    mid = residual + jnp.dot(attn_mix, out_full, preferred_element_type=jnp.float32)
    normed2, inv_rms2, hidden_n = norm_forward(mid, gain_m)
    gate = jnp.dot(hidden_n, gate_full, preferred_element_type=jnp.float32)
    up_val = jnp.dot(hidden_n, up_full, preferred_element_type=jnp.float32)
    sigma = jax.nn.sigmoid(gate)
    silu_gate = gate * sigma
    act = (silu_gate * up_val).astype(jnp.bfloat16)
    block_output = (mid + jnp.dot(act, down_full, preferred_element_type=jnp.float32)).astype(
        jnp.bfloat16
    )
    cotangent = out_cotangent[0]
    down_grad = transposed_times(act, cotangent)
    d_gate = (d_act * up_val * sigma * (1.0 + gate * (1.0 - sigma))).astype(jnp.bfloat16)
    d_up = (d_act * silu_gate).astype(jnp.bfloat16)
    gate_grad = transposed_times(hidden_n, d_gate)
    up_grad = transposed_times(hidden_n, d_up)
    d_hn = times_transposed(d_gate, gate_full) + times_transposed(d_up, up_full)
    mlp_gain_grad, d_norm2 = norm_backward(d_hn, normed2, inv_rms2, gain_m)
    d_mid = cotangent.astype(jnp.float32) + d_norm2
    d_mid_b = d_mid.astype(jnp.bfloat16)
    out_grad = transposed_times(attn_mix, d_mid_b)
    d_attn = times_transposed(d_mid_b, out_full).astype(jnp.bfloat16)
    d_queries, d_keys, d_values = attend_back(
        d_attn, attn_mix, query_rows, keys_three_axis, values_three_axis, visible, log_total
    )
    d_keys_flat = apply_rotation(d_keys, k_cos, k_sin, -1.0).reshape(every_length, key_columns)
    d_values_flat = d_values.reshape(every_length, key_columns)
    pair = jnp.concatenate([d_keys_flat, d_values_flat], axis=1)
    away = lax.dynamic_slice_in_dim(pair, row_span - offset, row_span)
    pair_part = lax.dynamic_slice_in_dim(pair, offset, row_span) + swap_halves(
        away.astype(jnp.bfloat16)
    ).astype(jnp.float32)
    d_proj = jnp.concatenate(
        [
            apply_rotation(d_queries, query_cosine, query_sine, -1.0).reshape(
                row_span, query_columns
            ),
            pair_part,
        ],
        axis=1,
    ).astype(jnp.bfloat16)
    qkv_grad = transposed_times(xn, d_proj)
    d_xn = times_transposed(d_proj, qkv_full)
    attn_gain_grad, d_norm1 = norm_backward(d_xn, normed1, inv_rms1, gain_a)
    input_grad = d_mid + d_norm1
    if copies == (2, 2):
        bf16 = jnp.bfloat16
        gain_grads = jnp.stack(
            [attn_gain_grad.reshape(ways, shard), mlp_gain_grad.reshape(ways, shard)], axis=1
        )
        gain_grads = jnp.pad(gain_grads, ((0, 0), (0, 14), (0, 512 - shard))).astype(bf16)
        width = d_mid_b.shape[1]
        both = (
            jnp.concatenate([xn, attn_mix], axis=0),
            jnp.concatenate(
                [
                    jnp.pad(d_proj, ((0, 0), (0, width))),
                    jnp.pad(d_mid_b, ((0, 0), (d_proj.shape[1], 0))),
                ],
                axis=0,
            ),
        )
        factors = [(hidden_n, d_gate), (hidden_n, d_up), (act, cotangent), both]
        gain_s, gate_s, up_s, down_s, both_s = reduce_shards(gain_grads, factors)
        qkv_s, out_s = both_s[:, : w_qkv.shape[1]], both_s[:, w_qkv.shape[1] :]
        gain_a_s, gain_m_s = gain_s[0, :shard], gain_s[1, :shard]
    else:
        grads = (attn_gain_grad, qkv_grad, out_grad, mlp_gain_grad, gate_grad, up_grad, down_grad)
        grads = [lax.psum_scatter(g, "fsdp", scatter_dimension=0, tiled=True) for g in grads]
        gain_a_s, qkv_s, out_s, gain_m_s, gate_s, up_s, down_s = lax.psum(grads, ("rep", "cp"))
    return (
        block_output[None],
        input_grad[None],
        gain_a_s,
        qkv_s,
        out_s,
        gain_m_s,
        gate_s,
        up_s,
        down_s,
    )


def solution(mesh):
    ways = mesh.shape["fsdp"]
    copies = (mesh.shape["rep"], mesh.shape["cp"])
    return jax.shard_map(
        functools.partial(shards, ways, copies),
        mesh=mesh,
        in_specs=(
            P(("fsdp", "rep"), "cp", None),
            P(("fsdp", "rep"), "cp"),
            P("fsdp"),
            P("fsdp", None),
            P("fsdp", None),
            P("fsdp"),
            P("fsdp", None),
            P("fsdp", None),
            P("fsdp", None),
            P(("fsdp", "rep"), "cp", None),
        ),
        out_specs=(
            P(("fsdp", "rep"), "cp", None),
            P(("fsdp", "rep"), "cp", None),
            P("fsdp"),
            P("fsdp", None),
            P("fsdp", None),
            P("fsdp"),
            P("fsdp", None),
            P("fsdp", None),
            P("fsdp", None),
        ),
        check_vma=False,
    )
```

```python
import functools

import jax
import jax.numpy as jnp
from jax import lax
from jax.experimental import pallas as pl
from jax.experimental.pallas import tpu as pltpu
from jax.sharding import PartitionSpec as P

QUERY_HEADS = 9
KEY_VALUE_HEADS = 3
HEAD_SIZE = 64


EPS = 1e-05
THETA = 100000.0
MASKED = -1e30

VMEM_BYTES = 50 * 1024 * 1024
MESH_ID = pl.DeviceIdType.MESH


def part_of(ref, lead, index, parts):
    rows, columns = ref.shape[-2:]
    if columns % (4 * 128) == 0:
        size = columns // parts
        return ref.at[lead, :, pl.ds(pl.multiple_of(index * size, size), size)]
    size = rows // parts
    return ref.at[lead, pl.ds(pl.multiple_of(index * size, size), size), :]


def gather_kernel(depth, count, *refs):
    ins, outs = refs[:count], refs[count : 2 * count]
    own_sem, z_send, z_recv, send1, recv1, send2, recv2, core_send, core_recv = refs[2 * count :]
    me, x, y = lax.axis_index("fsdp"), lax.axis_index("cp"), lax.axis_index("rep")
    z, core = me // 2, me % 2
    partner = 2 * z + 1 - core
    barrier = pltpu.get_barrier_semaphore()
    others = [{"fsdp": partner}, {"cp": 1 - x}, {"rep": 1 - y}]
    others += [{"fsdp": 2 * ((z + s) % depth) + core} for s in range(1, depth)]
    for other in others:
        pl.semaphore_signal(barrier, inc=1, device_id=other, device_id_type=MESH_ID)
    pl.semaphore_wait(barrier, len(others))

    def remote(source, place, send, recv, device):
        return pltpu.make_async_remote_copy(
            src_ref=source,
            dst_ref=place,
            send_sem=send,
            recv_sem=recv,
            device_id=device,
            device_id_type=MESH_ID,
        )

    def axes(j):
        return (x, y, "cp", "rep") if j % 2 == 0 else (y, x, "rep", "cp")

    def own(k):
        return pltpu.make_async_copy(ins[k].at[0], outs[k].at[me], own_sem.at[k])

    def outward(k, step):
        mine = jnp.where(z % 2 == 0, y * 2 + x, x * 2 + y)
        return remote(
            part_of(ins[k], 0, mine, 4),
            part_of(outs[k], me, mine, 4),
            z_send.at[k, step],
            z_recv.at[k, step],
            {"fsdp": 2 * ((z + step) % depth) + core},
        )

    def inward(k, step):
        shard = (z + depth - step) % depth
        even = shard % 2 == 0
        mine = jnp.where(even, y * 2 + x, x * 2 + y)
        place = part_of(outs[k], 2 * shard + core, mine, 4)
        return remote(place, place, z_send.at[k, step], z_recv.at[k, step], {"fsdp": partner})

    def joins(k, shard, which):
        own1, own2, name1, name2 = axes(shard)
        if which == 0:
            quarter = part_of(outs[k], 2 * shard + core, own2 * 2 + own1, 4)
            send, recv = send1.at[k, shard], recv1.at[k, shard]
            return remote(quarter, quarter, send, recv, {name1: 1 - own1})
        half = part_of(outs[k], 2 * shard + core, own2, 2)
        send, recv = send2.at[k, shard], recv2.at[k, shard]
        return remote(half, half, send, recv, {name2: 1 - own2})

    def across(k, shard, source=None):
        place = outs[k].at[2 * shard + core]
        return remote(
            place if source is None else source,
            place,
            core_send.at[k, shard],
            core_recv.at[k, shard],
            {"fsdp": partner},
        )

    for k in range(count):
        for step in range(1, depth):
            outward(k, step).start()
        own(k).start()
        across(k, z, ins[k].at[0]).start()

    def arrived(k, shard):
        step = (z + depth - shard) % depth

        @pl.when(shard != z)
        def _():
            inward(k, step).wait_recv()
            joins(k, shard, 0).start()

    def joined(k, shard):
        @pl.when(shard != z)
        def _():
            joins(k, shard, 0).wait_recv()
            joins(k, shard, 1).start()

    def complete(k, shard):
        @pl.when(shard != z)
        def _():
            joins(k, shard, 1).wait_recv()
            across(k, shard).start()

    items = [(k, shard) for k in range(count) for shard in range(depth)]
    lag = 2
    for t in range(len(items) + 2 * lag):
        for late, stage in ((0, arrived), (lag, joined), (2 * lag, complete)):
            if 0 <= t - late < len(items):
                stage(*items[t - late])
    for k in range(count):
        own(k).wait()
        for step in range(1, depth):
            outward(k, step).wait_send()
        for shard in range(depth):
            across(k, shard).wait_send()
            across(k, shard).wait_recv()

            @pl.when(shard != z)
            def _():
                joins(k, shard, 0).wait_send()
                joins(k, shard, 1).wait_send()


def gather_shards(arrays, ways):
    count, depth = len(arrays), ways // 2
    return pl.pallas_call(
        functools.partial(gather_kernel, depth, count),
        out_shape=[jax.ShapeDtypeStruct((ways,) + a.shape, a.dtype) for a in arrays],
        in_specs=[pl.BlockSpec(memory_space=pl.ANY)] * count,
        out_specs=[pl.BlockSpec(memory_space=pltpu.VMEM)] * count,
        scratch_shapes=[pltpu.SemaphoreType.DMA((count,))]
        + [pltpu.SemaphoreType.DMA((count, depth))] * 8,
        compiler_params=pltpu.CompilerParams(
            collective_id=1, has_side_effects=True, vmem_limit_bytes=VMEM_BYTES
        ),
    )(*[a[None] for a in arrays])


def reduce_kernel(depth, count, *refs):
    gains, factors, rest = refs[0], refs[1 : 2 * count - 1], refs[2 * count - 1 :]
    outs, products, rest = rest[:count], rest[count : 2 * count - 1], rest[2 * count - 1 :]
    parts = (gains,) + tuple(products)
    first, second, third, fourth, held, quarter, joined = [
        rest[i * count : (i + 1) * count] for i in range(7)
    ]
    send0, recv0, send1, recv1, send2, recv2, send3, recv3, send4, recv4 = rest[7 * count :]
    me, x, y = lax.axis_index("fsdp"), lax.axis_index("cp"), lax.axis_index("rep")
    z, core = me // 2, me % 2
    partner = 2 * z + 1 - core
    f32 = jnp.float32

    barrier = pltpu.get_barrier_semaphore()
    others = [{"fsdp": partner}, {"cp": 1 - x}, {"rep": 1 - y}, {"cp": 1 - x, "rep": 1 - y}]
    others += [{"fsdp": 2 * ((z + s) % depth) + core} for s in range(1, depth)]
    for other in others:
        pl.semaphore_signal(barrier, inc=1, device_id=other, device_id_type=MESH_ID)
    pl.semaphore_wait(barrier, len(others))

    def remote(source, place, send, recv, device):
        return pltpu.make_async_remote_copy(
            src_ref=source,
            dst_ref=place,
            send_sem=send,
            recv_sem=recv,
            device_id=device,
            device_id_type=MESH_ID,
        )

    def copy0(k, j):
        return remote(
            parts[k].at[2 * j + 1 - core],
            first[k].at[j],
            send0.at[k, j],
            recv0.at[k, j],
            {"fsdp": partner},
        )

    def axes(j):
        return (x, y, "cp", "rep") if j % 2 == 0 else (y, x, "rep", "cp")

    def copy1(k, j):
        own1, _, name1, _ = axes(j)
        return remote(
            part_of(held[k], j, 1 - own1, 2),
            second[k].at[j],
            send1.at[k, j],
            recv1.at[k, j],
            {name1: 1 - own1},
        )

    def copy2(k, j):
        own1, own2, _, name2 = axes(j)
        return remote(
            part_of(held[k], j, own1 * 2 + 1 - own2, 4),
            third[k].at[j],
            send2.at[k, j],
            recv2.at[k, j],
            {name2: 1 - own2},
        )

    def copy3(k, step):
        to = (z + step) % depth
        return remote(
            quarter[k].at[to],
            fourth[k].at[step],
            send3.at[k, step],
            recv3.at[k, step],
            {"fsdp": 2 * to + core},
        )

    mine = jnp.where(z % 2 == 0, x * 2 + y, y * 2 + x)

    def copy4(k, which):
        place = part_of(joined[k], 0, mine, 4)
        device = [{"cp": 1 - x}, {"rep": 1 - y}, {"cp": 1 - x, "rep": 1 - y}][which]
        return remote(place, place, send4.at[k, which], recv4.at[k, which], device)

    def multiply(k):
        if k > 0:
            left, right = factors[2 * k - 2], factors[2 * k - 1]
            ways, rows, columns = parts[k].shape
            contract = (((0,), (0,)), ((), ()))
            if columns % 512 == 0:

                def some_columns(n, carry):
                    span = pl.ds(pl.multiple_of(n * 512, 512), 512)
                    product = lax.dot_general(
                        left[...], right[:, span], contract, preferred_element_type=f32
                    )
                    for i in range(ways):
                        block = product[i * rows : (i + 1) * rows]
                        parts[k][i, :, span] = block.astype(parts[k].dtype)
                    return carry

                lax.fori_loop(0, columns // 512, some_columns, 0)
            else:

                def some_rows(n, carry):
                    span = pl.ds(pl.multiple_of(n * 2 * rows, 2 * rows), 2 * rows)
                    product = lax.dot_general(
                        left[:, span], right[...], contract, preferred_element_type=f32
                    )
                    for i in range(2):
                        block = product[i * rows : (i + 1) * rows]
                        parts[k][2 * n + i] = block.astype(parts[k].dtype)
                    return carry

                lax.fori_loop(0, ways // 2, some_rows, 0)
        for j in range(depth):
            copy0(k, j).start()

    def over_cores(k):
        for j in range(depth):
            copy0(k, j).wait_recv()
            total = parts[k][2 * j + core].astype(f32) + first[k][j].astype(f32)
            held[k][j] = total.astype(held[k].dtype)
            copy1(k, j).start()

    def over_first_axis(k):
        for j in range(depth):
            own1, _, _, _ = axes(j)
            copy1(k, j).wait_recv()
            half = part_of(held[k], j, own1, 2)
            half[...] = (half[...].astype(f32) + second[k][j].astype(f32)).astype(half.dtype)
            copy2(k, j).start()

    def over_second_axis(k):
        for j in range(depth):
            own1, own2, _, _ = axes(j)
            copy2(k, j).wait_recv()
            piece = part_of(held[k], j, own1 * 2 + own2, 4)
            total = piece[...].astype(f32) + third[k][j].astype(f32)
            quarter[k][j] = total.astype(quarter[k].dtype)
        for step in range(1, depth):
            copy3(k, step).start()

    def over_z(k):
        total = quarter[k][z].astype(f32)
        for step in range(1, depth):
            copy3(k, step).wait_recv()
            total = total + fourth[k][step].astype(f32)
        place = part_of(joined[k], 0, mine, 4)
        place[...] = total.astype(place.dtype)
        for which in range(3):
            copy4(k, which).start()

    def finish(k):
        for which in range(3):
            copy4(k, which).wait_recv()
        outs[k][...] = joined[k][0].astype(f32)

    stages = (multiply, over_cores, over_first_axis, over_second_axis, over_z, finish)
    for t in range(count + len(stages) - 1):
        for late, stage in enumerate(stages):
            if 0 <= t - late < count:
                stage(t - late)
    for k in range(count):
        for j in range(depth):
            copy0(k, j).wait_send()
            copy1(k, j).wait_send()
            copy2(k, j).wait_send()
        for step in range(1, depth):
            copy3(k, step).wait_send()
        for which in range(3):
            copy4(k, which).wait_send()


def reduce_shards(gains, factors):
    ways = gains.shape[0]
    depth, kind = ways // 2, gains.dtype
    arrays = [gains] + [
        jax.ShapeDtypeStruct((ways, left.shape[1] // ways, right.shape[1]), kind)
        for left, right in factors
    ]
    count = len(arrays)
    operands = [gains] + [f for pair in factors for f in pair]
    wholes = [(depth,) + a.shape[1:] for a in arrays]
    halves, quarters = [], []
    for a in arrays:
        rows, columns = a.shape[1:]
        by_columns = columns % (4 * 128) == 0
        halves.append((depth, rows, columns // 2) if by_columns else (depth, rows // 2, columns))
        quarters.append((depth, rows, columns // 4) if by_columns else (depth, rows // 4, columns))
    buffers = [pltpu.VMEM(a.shape, kind) for a in arrays[1:]]
    for shapes in (wholes, halves, quarters, quarters, wholes, quarters):
        buffers += [pltpu.VMEM(s, kind) for s in shapes]
    buffers += [pltpu.VMEM((1,) + a.shape[1:], kind) for a in arrays]
    sems = [pltpu.SemaphoreType.DMA((count, depth))] * 8 + [pltpu.SemaphoreType.DMA((count, 3))] * 2
    return pl.pallas_call(
        functools.partial(reduce_kernel, depth, count),
        out_shape=[jax.ShapeDtypeStruct(a.shape[1:], jnp.float32) for a in arrays],
        in_specs=[pl.BlockSpec(memory_space=pltpu.VMEM)] * len(operands),
        out_specs=[pl.BlockSpec(memory_space=pltpu.VMEM)] * count,
        scratch_shapes=buffers + sems,
        compiler_params=pltpu.CompilerParams(
            collective_id=2, has_side_effects=True, vmem_limit_bytes=VMEM_BYTES
        ),
    )(*operands)


def rope_tables(positions):
    half = HEAD_SIZE // 2
    freq = THETA ** (-2.0 * jnp.arange(half, dtype=jnp.float32) / HEAD_SIZE)
    angle = positions.astype(jnp.float32)[:, None] * freq[None, :]
    return (jnp.cos(angle), jnp.sin(angle))


def apply_rotation(tensor, cosine_table, sine_table, direction):
    half = HEAD_SIZE // 2
    first = tensor[..., :half]
    second = tensor[..., half:]
    cos_b = cosine_table[:, None, :]
    sin_b = sine_table[:, None, :] * direction
    return jnp.concatenate(
        [first * cos_b - second * sin_b, first * sin_b + second * cos_b], axis=-1
    )


def doc_positions(seg_row):
    index_row = jnp.arange(seg_row.shape[0], dtype=jnp.int32)
    starts = jnp.sum((seg_row[None, :] < seg_row[:, None]).astype(jnp.int32), axis=1)
    return index_row - starts


def times_transposed(left, right):
    return lax.dot_general(
        left, right, (((1,), (1,)), ((), ())), preferred_element_type=jnp.float32
    )


def transposed_times(left, right):
    return lax.dot_general(
        left, right, (((0,), (0,)), ((), ())), preferred_element_type=jnp.float32
    )


def norm_forward(values, gain):
    inv_rms = lax.rsqrt(jnp.mean(values * values, axis=-1, keepdims=True) + EPS)
    normed = values * inv_rms
    return (normed, inv_rms, (normed * gain.astype(jnp.float32)).astype(jnp.bfloat16))


def norm_backward(d_normed, normed, inv_rms, gain):
    gain_grad = jnp.sum(d_normed * normed, axis=0)
    scaled = d_normed * gain.astype(jnp.float32)
    return (
        gain_grad,
        inv_rms * (scaled - normed * jnp.mean(scaled * normed, axis=-1, keepdims=True)),
    )


def score_block(query_rows, keys_three_axis, visible):
    row_span = query_rows.shape[0]
    grouped_heads = query_rows.reshape(
        row_span, KEY_VALUE_HEADS, QUERY_HEADS // KEY_VALUE_HEADS, HEAD_SIZE
    )
    scores = jnp.einsum(
        "nkgd,mkd->kgnm", grouped_heads, keys_three_axis, preferred_element_type=jnp.float32
    ) * HEAD_SIZE ** (-0.5)
    return jnp.where(visible[None, None], scores, MASKED)


def attend(query_rows, keys_three_axis, values_three_axis, visible):
    row_span = query_rows.shape[0]
    scores = score_block(query_rows, keys_three_axis, visible)
    top = jnp.max(scores, axis=-1, keepdims=True)
    expo = jnp.exp(scores - top)
    total = jnp.sum(expo, axis=-1, keepdims=True)
    probs = (expo / total).astype(jnp.bfloat16)
    log_total = top + jnp.log(total)
    mixed_heads = jnp.einsum(
        "kgnm,mkd->nkgd", probs, values_three_axis, preferred_element_type=jnp.float32
    )
    return (mixed_heads.reshape(row_span, QUERY_HEADS * HEAD_SIZE).astype(jnp.bfloat16), log_total)


def attend_back(
    mixed_gradient, mixed_heads, query_rows, keys_three_axis, values_three_axis, visible, log_total
):
    row_span = query_rows.shape[0]
    query_group = QUERY_HEADS // KEY_VALUE_HEADS
    scores = score_block(query_rows, keys_three_axis, visible)
    probs = jnp.exp(scores - log_total)
    probs_b = probs.astype(jnp.bfloat16)
    grouped_gradient = mixed_gradient.reshape(row_span, KEY_VALUE_HEADS, query_group, HEAD_SIZE)
    d_values = jnp.einsum(
        "kgnm,nkgd->mkd", probs_b, grouped_gradient, preferred_element_type=jnp.float32
    )
    d_probs = jnp.einsum(
        "nkgd,mkd->kgnm", grouped_gradient, values_three_axis, preferred_element_type=jnp.float32
    )
    change_amount = jnp.sum(
        grouped_gradient.astype(jnp.float32)
        * mixed_heads.reshape(row_span, KEY_VALUE_HEADS, query_group, HEAD_SIZE).astype(
            jnp.float32
        ),
        axis=-1,
    )
    change_amount = jnp.transpose(change_amount, (1, 2, 0))[..., None]
    d_scores = (probs * (d_probs - change_amount)).astype(jnp.bfloat16)
    grouped_heads = query_rows.reshape(row_span, KEY_VALUE_HEADS, query_group, HEAD_SIZE)
    d_queries = jnp.einsum(
        "kgnm,mkd->nkgd", d_scores, keys_three_axis, preferred_element_type=jnp.float32
    ) * HEAD_SIZE ** (-0.5)
    d_keys = jnp.einsum(
        "kgnm,nkgd->mkd", d_scores, grouped_heads, preferred_element_type=jnp.float32
    ) * HEAD_SIZE ** (-0.5)
    return (d_queries.reshape(row_span, QUERY_HEADS, HEAD_SIZE), d_keys, d_values)


def swap_halves(value):
    return lax.ppermute(value, "cp", [(0, 1), (1, 0)])


def both_halves(value, axis):
    other = swap_halves(value)
    first = lax.axis_index("cp") == 0
    return jnp.concatenate(
        [jnp.where(first, value, other), jnp.where(first, other, value)], axis=axis
    )


def shards(
    ways, copies, block_input, segment_ids, attn_gain, w_qkv, w_out, mlp_gain, w_gate, w_up, w_down, out_cotangent
):
    residual = block_input[0].astype(jnp.float32)
    row_span = residual.shape[0]
    query_columns = QUERY_HEADS * HEAD_SIZE
    key_columns = KEY_VALUE_HEADS * HEAD_SIZE
    shard = attn_gain.shape[0]
    gains = jnp.zeros((16, 512), jnp.bfloat16)
    gains = gains.at[0, :shard].set(attn_gain).at[1, :shard].set(mlp_gain)
    own_weights = [jnp.concatenate([w_qkv, w_out], axis=1), gains, w_gate, w_up, w_down]
    if copies == (2, 2):
        gathered = gather_shards(own_weights, ways)
    else:
        gathered = [lax.all_gather(w, "fsdp") for w in own_weights]
    both_full, gate_full, up_full, down_full = [
        gathered[i].reshape(-1, gathered[i].shape[-1]) for i in (0, 2, 3, 4)
    ]
    qkv_full, out_full = both_full[:, : w_qkv.shape[1]], both_full[:, w_qkv.shape[1] :]
    gain_a = gathered[1][:, 0, :shard].reshape(-1)
    gain_m = gathered[1][:, 1, :shard].reshape(-1)
    whole_ids = both_halves(segment_ids, 1)[0]
    every_length = whole_ids.shape[0]
    offset = lax.axis_index("cp") * row_span
    key_index = jnp.arange(every_length, dtype=jnp.int32)
    key_positions = doc_positions(whole_ids)
    query_index = offset + jnp.arange(row_span, dtype=jnp.int32)
    query_positions = lax.dynamic_slice_in_dim(key_positions, offset, row_span)
    local_ids = segment_ids[0]
    visible = (whole_ids[None, :] == local_ids[:, None]) & (
        key_index[None, :] <= query_index[:, None]
    )
    query_cosine, query_sine = rope_tables(query_positions)
    k_cos, k_sin = rope_tables(key_positions)
    normed1, inv_rms1, xn = norm_forward(residual, gain_a)
    output_projection = jnp.dot(xn, qkv_full, preferred_element_type=jnp.float32)
    query_rows = apply_rotation(
        output_projection[:, :query_columns].reshape(row_span, QUERY_HEADS, HEAD_SIZE),
        query_cosine,
        query_sine,
        1.0,
    ).astype(jnp.bfloat16)
    keys_local = (
        apply_rotation(
            output_projection[:, query_columns : query_columns + key_columns].reshape(
                row_span, KEY_VALUE_HEADS, HEAD_SIZE
            ),
            query_cosine,
            query_sine,
            1.0,
        )
        .astype(jnp.bfloat16)
        .reshape(row_span, key_columns)
    )
    values_local = output_projection[:, query_columns + key_columns :].astype(jnp.bfloat16)
    every_pair = both_halves(jnp.concatenate([keys_local, values_local], axis=1), 0)
    every_key, every_value = every_pair[:, :key_columns], every_pair[:, key_columns:]
    keys_three_axis = every_key.reshape(every_length, KEY_VALUE_HEADS, HEAD_SIZE)
    values_three_axis = every_value.reshape(every_length, KEY_VALUE_HEADS, HEAD_SIZE)
    attn_mix, log_total = attend(query_rows, keys_three_axis, values_three_axis, visible)
    mid = residual + jnp.dot(attn_mix, out_full, preferred_element_type=jnp.float32)
    normed2, inv_rms2, hidden_n = norm_forward(mid, gain_m)
    gate = jnp.dot(hidden_n, gate_full, preferred_element_type=jnp.float32)
    up_val = jnp.dot(hidden_n, up_full, preferred_element_type=jnp.float32)
    sigma = jax.nn.sigmoid(gate)
    silu_gate = gate * sigma
    act = (silu_gate * up_val).astype(jnp.bfloat16)
    block_output = (mid + jnp.dot(act, down_full, preferred_element_type=jnp.float32)).astype(
        jnp.bfloat16
    )
    cotangent = out_cotangent[0]
    d_act = times_transposed(cotangent, down_full)
    down_grad = transposed_times(act, cotangent)
    d_gate = (d_act * up_val * sigma * (1.0 + gate * (1.0 - sigma))).astype(jnp.bfloat16)
    d_up = (d_act * silu_gate).astype(jnp.bfloat16)
    gate_grad = transposed_times(hidden_n, d_gate)
    up_grad = transposed_times(hidden_n, d_up)
    d_hn = times_transposed(d_gate, gate_full) + times_transposed(d_up, up_full)
    mlp_gain_grad, d_norm2 = norm_backward(d_hn, normed2, inv_rms2, gain_m)
    d_mid = cotangent.astype(jnp.float32) + d_norm2
    d_mid_b = d_mid.astype(jnp.bfloat16)
    out_grad = transposed_times(attn_mix, d_mid_b)
    d_attn = times_transposed(d_mid_b, out_full).astype(jnp.bfloat16)
    d_queries, d_keys, d_values = attend_back(
        d_attn, attn_mix, query_rows, keys_three_axis, values_three_axis, visible, log_total
    )
    d_keys_flat = apply_rotation(d_keys, k_cos, k_sin, -1.0).reshape(every_length, key_columns)
    d_values_flat = d_values.reshape(every_length, key_columns)
    pair = jnp.concatenate([d_keys_flat, d_values_flat], axis=1)
    away = lax.dynamic_slice_in_dim(pair, row_span - offset, row_span)
    pair_part = lax.dynamic_slice_in_dim(pair, offset, row_span) + swap_halves(
        away.astype(jnp.bfloat16)
    ).astype(jnp.float32)
    d_proj = jnp.concatenate(
        [
            apply_rotation(d_queries, query_cosine, query_sine, -1.0).reshape(
                row_span, query_columns
            ),
            pair_part,
        ],
        axis=1,
    ).astype(jnp.bfloat16)
    qkv_grad = transposed_times(xn, d_proj)
    d_xn = times_transposed(d_proj, qkv_full)
    attn_gain_grad, d_norm1 = norm_backward(d_xn, normed1, inv_rms1, gain_a)
    input_grad = d_mid + d_norm1
    if copies == (2, 2):
        bf16 = jnp.bfloat16
        gain_grads = jnp.stack(
            [attn_gain_grad.reshape(ways, shard), mlp_gain_grad.reshape(ways, shard)], axis=1
        )
        gain_grads = jnp.pad(gain_grads, ((0, 0), (0, 14), (0, 512 - shard))).astype(bf16)
        width = d_mid_b.shape[1]
        both = (
            jnp.concatenate([xn, attn_mix], axis=0),
            jnp.concatenate(
                [
                    jnp.pad(d_proj, ((0, 0), (0, width))),
                    jnp.pad(d_mid_b, ((0, 0), (d_proj.shape[1], 0))),
                ],
                axis=0,
            ),
        )
        factors = [(hidden_n, d_gate), (hidden_n, d_up), (act, cotangent), both]
        gain_s, gate_s, up_s, down_s, both_s = reduce_shards(gain_grads, factors)
        qkv_s, out_s = both_s[:, : w_qkv.shape[1]], both_s[:, w_qkv.shape[1] :]
        gain_a_s, gain_m_s = gain_s[0, :shard], gain_s[1, :shard]
    else:
        grads = (attn_gain_grad, qkv_grad, out_grad, mlp_gain_grad, gate_grad, up_grad, down_grad)
        grads = [lax.psum_scatter(g, "fsdp", scatter_dimension=0, tiled=True) for g in grads]
        gain_a_s, qkv_s, out_s, gain_m_s, gate_s, up_s, down_s = lax.psum(grads, ("rep", "cp"))
    return (
        block_output[None],
        input_grad[None],
        gain_a_s,
        qkv_s,
        out_s,
        gain_m_s,
        gate_s,
        up_s,
        down_s,
    )


def solution(mesh):
    ways = mesh.shape["fsdp"]
    copies = (mesh.shape["rep"], mesh.shape["cp"])
    return jax.shard_map(
        functools.partial(shards, ways, copies),
        mesh=mesh,
        in_specs=(
            P(("fsdp", "rep"), "cp", None),
            P(("fsdp", "rep"), "cp"),
            P("fsdp"),
            P("fsdp", None),
            P("fsdp", None),
            P("fsdp"),
            P("fsdp", None),
            P("fsdp", None),
            P("fsdp", None),
            P(("fsdp", "rep"), "cp", None),
        ),
        out_specs=(
            P(("fsdp", "rep"), "cp", None),
            P(("fsdp", "rep"), "cp", None),
            P("fsdp"),
            P("fsdp", None),
            P("fsdp", None),
            P("fsdp"),
            P("fsdp", None),
            P("fsdp", None),
            P("fsdp", None),
        ),
        check_vma=False,
    )
```
